32 devices in a mesh: seq: 4 (over y, core), exp: 8 (over z, x).
Axes of the slice: x: 2, y: 2, z: 4, core: 2. Of those that a mesh axis runs over, the one named last changes fastest.
Arguments:
- layer_input: bfloat16 [8, 1024, 2048], P('exp', 'seq'), may hold values from -6 to 6
- queries: bfloat16 [8, 1024, 2048], P('exp', 'seq'), may hold values from -6 to 6
- keys_in: bfloat16 [8, 1024, 2048], P('exp', 'seq'), may hold values from -0.59765625 to 0.59765625
- values_in: bfloat16 [8, 1024, 2048], P('exp', 'seq'), may hold values from -6 to 6
- decay_rate: float32 [8, 1024, 16], P('exp', 'seq'), as said below
- attn_gain: float32 [2048], replicated, may hold values from 0.25 to 1.75
- norm_gain: float32 [2048], replicated, may hold values from 0.25 to 1.75
- expert_ids: int32 [8, 1024, 2], P('exp', 'seq'), may hold values from 0 to 7, all different within a row; in each aligned block of 256 rows (0 to 255, 256 to 511, ..., all dimensions but the last counted through in order) at most 96 rows name the same one
- gate_levels: int32 [8, 1024, 2], P('exp', 'seq'), may hold values from 1 to 256
- w_gate: bfloat16 [8, 2048, 768], P('exp'), may hold values from -0.125 to 0.125
- w_up: bfloat16 [8, 2048, 768], P('exp'), may hold values from -0.125 to 0.125
- w_down: bfloat16 [8, 768, 2048], P('exp'), may hold values from -0.21875 to 0.21875
Outputs:
- layer_out: bfloat16 [8, 1024, 2048], P('exp', 'seq')
The draws below stay inside these ranges and needn't reach their ends.
Inputs may be any that keep to these rules, and one draw needn't show every extreme that they name: `expert_ids`: each token names 2 different experts. Among the 256 positions of one device, no expert is named by more than 96 routes, a bound that some block reaches. `decay_rate`: every entry is positive.
All inputs are finite; a program needn't handle non-finite values.
Results may differ from the reference program's by a relative error of at most 0.01.
Values may be sent and summed in bfloat16 or wider, within the bound.
A program may use at most 128 MiB of HBM per device.

```python
import math
import jax
import jax.numpy as jnp
import numpy as np
from jax import lax

D = 2048
HEADS = 16
DH = 128
FF = 768
TOP = 2
TOK_DEV = 256
EXPERTS = 8
CAP = 96
SEQUENCE_COUNT = 8
SEQUENCE_LENGTH = 1024
N_SEQ = 4


def draw_decay_rate(key, part):
    random_key_list = jax.random.split(key, 7)
    full_shape = (SEQUENCE_COUNT, SEQUENCE_LENGTH, HEADS)
    fast_share = 0.5
    fast_head = jax.random.uniform(random_key_list[0], (SEQUENCE_COUNT, 1, HEADS)) < fast_share
    slow_total = jax.random.uniform(random_key_list[1], (SEQUENCE_COUNT, 1, HEADS), minval=0.05, maxval=0.25)
    block_count = SEQUENCE_LENGTH // TOK_DEV
    block_factor = 2.0 ** jax.random.uniform(random_key_list[2], (SEQUENCE_COUNT, block_count, HEADS), minval=-1.0, maxval=1.0)
    block_factor = jnp.repeat(block_factor, TOK_DEV, axis=1)
    rough_factor = jax.random.uniform(random_key_list[3], full_shape, minval=0.5, maxval=1.5)
    slow_rate = slow_total / SEQUENCE_LENGTH * block_factor * rough_factor
    fast_rate = rough_factor / jax.random.uniform(random_key_list[4], (SEQUENCE_COUNT, 1, HEADS), minval=30.0, maxval=50.0)
    baseline_rate = jnp.where(fast_head, fast_rate, slow_rate)
    spike_positions = jax.random.randint(random_key_list[5], (SEQUENCE_COUNT, 2), 0, SEQUENCE_LENGTH)
    draw_amount = jax.random.uniform(random_key_list[6], (SEQUENCE_COUNT, 2), minval=0.22, maxval=0.6)
    position_indices = jnp.arange(SEQUENCE_LENGTH)[None, :, None]
    spike_rate = jnp.sum(jnp.where(position_indices == spike_positions[:, None, :], draw_amount[:, None, :], 0.0), axis=2)
    return (baseline_rate + spike_rate[:, :, None]).astype(jnp.float32)


def place_ends(values, rng, least, high):
    shape = values.shape
    place = [jax.random.randint(jax.random.fold_in(rng, axis), (), 0, shape[axis]) for axis in range(len(shape))]
    values = values.at[tuple(place)].set(least)
    longest = shape.index(max(shape))
    place[longest] = (place[longest] + 1) % shape[longest]
    return values.at[tuple(place)].set(high)


def level_of(rng, shape, cuts, least, high):
    loudness, own = 1.0, jax.random.fold_in(rng, 6)
    for axis_at, shards_of in cuts:
        steps = jnp.exp(jax.random.uniform(jax.random.fold_in(own, axis_at), (shards_of,), jnp.float32, least / len(cuts), high / len(cuts)))
        loudness = loudness * jnp.repeat(steps, shape[axis_at] // shards_of).reshape([-1 if axis == axis_at else 1 for axis in range(len(shape))])
    return loudness


def deal_out(rng, own, number, rows, count, top, limit, slope):
    sequence = jax.random.permutation(rng, count)
    heavy_load, usual = shares(count, rows * top, limit, slope, True), shares(count, rows * top, limit, slope, False)
    places = jnp.arange(count)

    def named(lengths, offset_by):
        used = int((lengths > 0).sum())
        fixed = max(1, used // 4)
        passed = fixed + (places - fixed + offset_by * (used - fixed)) % max(1, count - fixed)
        return jnp.zeros((count,), jnp.int32).at[sequence[jnp.where(places < fixed, places, passed)]].set(jnp.asarray(lengths, jnp.int32))

    lengths = jnp.where(number % 4 == 0, named(heavy_load, number // 4), named(usual, number - number // 4 - 1))
    mixed = jax.random.permutation(jax.random.fold_in(own, 3), count)
    source_of, receiver = mixed[0:count // 2 * 2:2], mixed[1:count // 2 * 2:2]
    margin = jnp.minimum(lengths[source_of] - 1, limit - lengths[receiver]) // 2
    margin = jnp.where((source_of == sequence[0]) | (receiver == sequence[0]) | (lengths[receiver] == 0), 0, jnp.maximum(margin, 0))
    passed = jax.random.randint(jax.random.fold_in(own, 4), (count // 2,), 0, 1 << 20) % (margin + 1)
    lengths = lengths.at[source_of].add(-passed).at[receiver].add(passed)
    members = jnp.searchsorted(jnp.cumsum(lengths), jnp.arange(rows * top), side="right").astype(jnp.int32)
    grid = members.reshape(top, rows).T
    grid = grid[jax.random.permutation(jax.random.fold_in(own, 1), rows)]
    offset_by = jax.random.randint(jax.random.fold_in(own, 2), (rows, 1), 0, top)
    return jnp.take_along_axis(grid, (jnp.arange(top)[None, :] + offset_by) % top, axis=1)


def shares(amount, total, most, slope, full):
    weights = [(1 << 20) // math.isqrt(standing ** slope) + 1 for standing in range(1, amount + 1)]
    largest = most if full else min(most, max(-(-total // amount), total * weights[0] // sum(weights)))
    least = 1 if total - largest >= amount - 1 else 0
    holding, rest = [largest] + [least] * (amount - 1), total - largest - least * (amount - 1)
    while rest > 0:
        movable = [i for i in range(1, amount) if holding[i] < largest] or [i for i in range(1, amount) if holding[i] < most]
        whole, budget = sum([weights[i] for i in movable]), rest
        for i in movable:
            more = min(most - holding[i], max(1, budget * weights[i] // whole), rest)
            holding[i] = holding[i] + more
            rest = rest - more
    return np.array(holding)


def noise(key, dims, spread, limit, shards=(), kind=jnp.bfloat16):
    entries = spread * jax.random.normal(key, dims, jnp.float32)
    if shards:
        entries = entries * level_of(key, dims, shards, -0.22, 0.18)
    return jnp.clip(entries, -limit, limit).astype(kind)


def setup_inputs(seed: int = 0) -> dict:
    seeds = jax.random.split(jax.random.key(seed), 13)
    layer_input = noise(seeds[0], (SEQUENCE_COUNT, SEQUENCE_LENGTH, D), 1.0, 6.0, ((0, 8), (1, 4)))
    queries = noise(seeds[1], (SEQUENCE_COUNT, SEQUENCE_LENGTH, D), 1.0, 6.0, ((0, 8), (1, 4)))
    keys_in = noise(seeds[2], (SEQUENCE_COUNT, SEQUENCE_LENGTH, D), 0.0884, 0.59765625, ((0, 8), (1, 4)))
    values_in = noise(seeds[3], (SEQUENCE_COUNT, SEQUENCE_LENGTH, D), 1.0, 6.0, ((0, 8), (1, 4)))
    decay_rate = draw_decay_rate(jax.random.fold_in(seeds[12], 71), 0)
    attn_gain = jnp.clip(1.0 + 0.15 * jax.random.normal(seeds[5], (D,), jnp.float32), 0.25, 1.75)
    norm_gain = jnp.clip(1.0 + 0.15 * jax.random.normal(seeds[6], (D,), jnp.float32), 0.25, 1.75)
    expert_ids_keys = jax.random.split(jax.random.fold_in(seeds[7], 1), SEQUENCE_COUNT * SEQUENCE_LENGTH // TOK_DEV)
    expert_ids_turns = jax.random.permutation(jax.random.fold_in(seeds[7], 3), SEQUENCE_COUNT * SEQUENCE_LENGTH // TOK_DEV)
    expert_ids = jax.vmap(lambda own, number: deal_out(jax.random.fold_in(seeds[7], 2), own, number, TOK_DEV, EXPERTS, TOP, CAP, 1))(expert_ids_keys, expert_ids_turns).reshape((SEQUENCE_COUNT, SEQUENCE_LENGTH, TOP))
    gate_levels = place_ends(jax.random.randint(seeds[8], (SEQUENCE_COUNT, SEQUENCE_LENGTH, TOP), 1, 257), jax.random.fold_in(seeds[8], 1), 1, 256).astype(jnp.int32)
    w_gate = noise(seeds[9], (EXPERTS, D, FF), D ** -0.5, 0.125, ((0, 8),))
    w_up = noise(seeds[10], (EXPERTS, D, FF), D ** -0.5, 0.125, ((0, 8),))
    w_down = noise(seeds[11], (EXPERTS, FF, D), FF ** -0.5, 0.21875, ((0, 8),))
    return dict(layer_input=layer_input, queries=queries, keys_in=keys_in, values_in=values_in, decay_rate=decay_rate, attn_gain=attn_gain, norm_gain=norm_gain, expert_ids=expert_ids, gate_levels=gate_levels, w_gate=w_gate, w_up=w_up, w_down=w_down)


def attend_block(carried, block_data):
    query_block, key_block, value_block, decay_block = block_data
    block_len = query_block.shape[0]
    cumulative = -jnp.cumsum(decay_block, axis=0)
    block_total = cumulative[-1]
    query_heads = query_block.reshape(block_len, HEADS, DH).astype(jnp.float32)
    key_heads = key_block.reshape(block_len, HEADS, DH).astype(jnp.float32)
    value_heads = value_block.reshape(block_len, HEADS, DH).astype(jnp.float32)
    scores = jnp.einsum('thd,shd->hts', query_heads, key_heads)
    cum_heads = cumulative.T
    log_gap = cum_heads[:, :, None] - cum_heads[:, None, :]
    row_index = jnp.arange(block_len)[:, None]
    col_index = jnp.arange(block_len)[None, :]
    causal = (row_index >= col_index)[None]
    weights = jnp.where(causal, jnp.exp(jnp.minimum(log_gap, 0.0)), 0.0)
    attn_probs = (scores * weights).astype(jnp.bfloat16)
    intra_part = jnp.einsum('hts,shd->thd', attn_probs.astype(jnp.float32), value_heads)
    inter_part = jnp.exp(cumulative)[:, :, None] * jnp.einsum('thd,hde->the', query_heads, carried, precision=lax.Precision.HIGHEST)
    key_weighted = key_heads * jnp.exp(block_total[None, :] - cumulative)[:, :, None]
    contrib = jnp.einsum('thd,the->hde', key_weighted, value_heads, precision=lax.Precision.HIGHEST)
    new_state = jnp.exp(block_total)[:, None, None] * carried + contrib
    return (new_state, intra_part + inter_part)

def one_sequence(seq_args):
    seq_query, seq_keys, seq_values, seq_decay = seq_args
    blocks = (seq_query.reshape(N_SEQ, TOK_DEV, D), seq_keys.reshape(N_SEQ, TOK_DEV, D), seq_values.reshape(N_SEQ, TOK_DEV, D), seq_decay.reshape(N_SEQ, TOK_DEV, HEADS))
    zero_state = jnp.zeros((HEADS, DH, DH), jnp.float32)
    final_state, outputs = lax.scan(attend_block, zero_state, blocks)
    return outputs.reshape(SEQUENCE_LENGTH, HEADS, DH)

def reference(layer_input, queries, keys_in, values_in, decay_rate, attn_gain, norm_gain, expert_ids, gate_levels, w_gate, w_up, w_down):
    raw_attn = lax.map(one_sequence, (queries, keys_in, values_in, decay_rate))
    normed_heads = raw_attn / jnp.sqrt(lax.optimization_barrier(jnp.mean(raw_attn * raw_attn, axis=-1, keepdims=True)) + 1e-06)
    h_res = layer_input.astype(jnp.float32) + normed_heads.reshape(SEQUENCE_COUNT, SEQUENCE_LENGTH, D) * attn_gain
    normed = (norm_gain * h_res / jnp.sqrt(lax.optimization_barrier(jnp.mean(h_res * h_res, axis=-1, keepdims=True)) + 1e-06)).astype(jnp.bfloat16)
    row_count = SEQUENCE_COUNT * SEQUENCE_LENGTH
    routed = jnp.repeat(normed.reshape(row_count, D), TOP, axis=0)
    flat_ids = expert_ids.reshape(-1).astype(jnp.int32)
    gate_scale = gate_levels.reshape(-1).astype(jnp.float32) / 256.0
    slots_total = SEQUENCE_COUNT * N_SEQ * CAP

    def per_expert(accum_out, expert_item):
        expert, weight_gate, weight_up, weight_down = expert_item
        chosen = flat_ids == expert
        position = jnp.cumsum(chosen.astype(jnp.int32)) - 1
        slot_index = jnp.where(chosen, position, slots_total).astype(jnp.int32)
        buffer = jnp.zeros((slots_total, D), jnp.bfloat16).at[slot_index].set(routed, mode='drop')
        gate_part = jnp.dot(buffer, weight_gate, preferred_element_type=jnp.float32)
        up_part = jnp.dot(buffer, weight_up, preferred_element_type=jnp.float32)
        activation = (jax.nn.silu(gate_part) * up_part).astype(jnp.bfloat16)
        result = jnp.dot(activation, weight_down, preferred_element_type=jnp.float32).astype(jnp.bfloat16)
        picked = result[jnp.minimum(slot_index, slots_total - 1)].astype(jnp.float32)
        accum_out = accum_out + jnp.where(chosen, gate_scale, 0.0)[:, None] * picked
        return (accum_out, None)
    zero_out = jnp.zeros((row_count * TOP, D), jnp.float32)
    accum_out, unused = lax.scan(per_expert, zero_out, (jnp.arange(EXPERTS, dtype=jnp.int32), w_gate, w_up, w_down))
    moe_out = lax.optimization_barrier(jnp.sum(accum_out.reshape(row_count, TOP, D), axis=1))
    return (h_res + moe_out.reshape(SEQUENCE_COUNT, SEQUENCE_LENGTH, D)).astype(jnp.bfloat16)
```

```python
import functools

import jax
import jax.numpy as jnp
from jax import lax
from jax.experimental import pallas as pl
from jax.experimental.pallas import tpu as pltpu
from jax.sharding import PartitionSpec as P

MESH = pl.DeviceIdType.MESH
F32 = jnp.float32
BF16 = jnp.bfloat16


def flip(index, mask, bits):
    result = 0
    for b in range(bits):
        p = 1 << b
        result = result + p * lax.rem(lax.div(index, p) + lax.div(mask, p), 2)
    return result


def dot(a, b, contract=((1,), (0,)), **kw):
    return lax.dot_general(a, b, (contract, ((), ())), preferred_element_type=F32, **kw)


def layer_kernel(
    dims,
    x_ref,
    q_ref,
    k_ref,
    v_ref,
    decay_ref,
    attn_gain_ref,
    norm_gain_ref,
    ids_ref,
    levels_ref,
    wg_hbm,
    wu_hbm,
    wd_hbm,
    out_ref,
    wg,
    wu,
    wd,
    cum,
    cum_rows,
    logs,
    logs_before,
    contrib,
    state_out,
    pair_in,
    state_in,
    carried,
    h_res,
    normed,
    pick,
    mix,
    send,
    recv,
    act,
    done,
    back,
    weight_sem,
    pair_sem,
    log_sem,
    state_send_sem,
    state_recv_sem,
    go_send_sem,
    go_recv_sem,
    back_send_sem,
    back_recv_sem,
):
    owners, cap, seqs, heads, top = dims
    block_len, width = x_ref.shape
    dh = width // heads
    ff = wg.shape[1]
    bits = owners.bit_length() - 1
    seq = lax.axis_index("seq")
    mine = lax.axis_index("exp")
    chip = lax.div(seq, 2)
    core = lax.rem(seq, 2)

    weight_copies = [
        pltpu.make_async_copy(hbm, vmem, weight_sem.at[i])
        for i, (hbm, vmem) in enumerate(((wg_hbm, wg), (wu_hbm, wu), (wd_hbm, wd)))
    ]
    for copy in weight_copies:
        copy.start()

    barrier = pltpu.get_barrier_semaphore()
    for step in range(1, seqs):
        pl.semaphore_signal(
            barrier, inc=1, device_id={"seq": lax.rem(seq + step, seqs)}, device_id_type=MESH
        )
    for step in range(1, owners):
        pl.semaphore_signal(
            barrier, inc=1, device_id={"exp": lax.rem(mine + step, owners)}, device_id_type=MESH
        )

    down = lax.broadcasted_iota(jnp.int32, (block_len, block_len), 0)
    across = lax.broadcasted_iota(jnp.int32, (block_len, block_len), 1)
    lower = (down >= across).astype(F32)
    upper = (down <= across).astype(F32)
    rate = -decay_ref[...]
    cum[...] = dot(lower, rate, precision=lax.Precision.HIGHEST)
    cum_rows[...] = dot(rate, upper, ((0,), (0,)), precision=lax.Precision.HIGHEST)
    logs[...] = jnp.broadcast_to(cum_rows[:, block_len - 1 : block_len], logs.shape)
    lanes = lax.broadcasted_iota(jnp.int32, (block_len, heads), 1)

    def head_cum(h):
        return jnp.sum(jnp.where(lanes == h, cum[...], 0.0), axis=1, keepdims=True)

    def head_lanes(h):
        return pl.ds(pl.multiple_of(h * dh, dh), dh)

    def contrib_head(h, _):
        c = head_cum(h)
        cols = head_lanes(h)
        weight = jnp.exp(c[block_len - 1 :, :] - c)
        weighted = (k_ref[:, cols].astype(F32) * weight).astype(BF16)
        value = dot(weighted, v_ref[:, cols], ((0,), (0,)))
        contrib[h] = value
        state_out[h] = value.astype(BF16)
        return 0

    lax.fori_loop(0, heads, contrib_head, 0)
    pl.semaphore_wait(barrier, seqs - 1 + owners - 1)

    def pair_copy(target):
        return pltpu.make_async_remote_copy(
            state_out, pair_in, pair_sem.at[0], pair_sem.at[1], {"seq": target}, MESH
        )

    def log_copy(target):
        return pltpu.make_async_remote_copy(
            logs, logs_before, log_sem.at[0], log_sem.at[1], {"seq": target}, MESH
        )

    def state_copy(step):
        return pltpu.make_async_remote_copy(
            state_out,
            state_in,
            state_send_sem.at[step - 1],
            state_recv_sem,
            {"seq": lax.rem(seq + step, seqs)},
            MESH,
        )

    @pl.when(core == 0)
    def _():
        pair_copy(seq + 1).start()
        log_copy(seq + 1).start()

    expert = lax.broadcasted_iota(jnp.int32, (block_len, owners), 1)
    named = [ids_ref[:, i : i + 1] == expert for i in range(top)]
    member = sum(n.astype(F32) for n in named)
    member_bf = member.astype(BF16)
    before = (down > across).astype(BF16)
    after = (down < across).astype(BF16)
    same = (down == across).astype(BF16)
    rank = dot(before, member_bf)
    rank_rows = dot(member_bf, after, ((0,), (0,)))
    member_rows = dot(member_bf, same, ((0,), (0,)))
    place_rows = jnp.where(member_rows > 0.5, rank_rows, -1.0)
    slot = lax.broadcasted_iota(jnp.int32, (cap, block_len), 0).astype(F32)
    for e in range(owners):
        pick[e] = jnp.where(place_rows[e : e + 1, :] == slot, 1.0, 0.0).astype(BF16)
    row = rank + expert.astype(F32) * cap
    column = lax.broadcasted_iota(jnp.int32, (block_len, owners * cap), 1).astype(F32)
    total = jnp.zeros((block_len, owners * cap), F32)
    for i in range(top):
        at = jnp.sum(jnp.where(named[i], row, 0.0), axis=1, keepdims=True)
        level = levels_ref[:, i : i + 1].astype(F32) * (1.0 / 256.0)
        total = total + jnp.where(column == at, level, 0.0)
    mix[...] = total.astype(BF16)

    def decay_row(ref, h):
        return jnp.exp(ref[pl.ds(h, 1), :])

    @pl.when(core == 1)
    def _():
        pair_copy(seq).wait_recv()
        log_copy(seq).wait_recv()

        def add_pair(h, _):
            both = decay_row(logs, h) * pair_in[h].astype(F32) + contrib[h]
            contrib[h] = both
            state_out[h] = both.astype(BF16)
            return 0

        lax.fori_loop(0, heads, add_pair, 0)

        @pl.when((chip == 0) & (seqs > 2))
        def _():
            for step in (1, 2):
                state_copy(step).start()

    def intra_head(h, _):
        c = head_cum(h)
        cols = head_lanes(h)
        scores = dot(q_ref[:, cols], k_ref[:, cols], ((1,), (1,)))
        gap = c - cum_rows[pl.ds(h, 1), :]
        weight = jnp.where(down >= across, jnp.exp(jnp.minimum(gap, 0.0)), 0.0)
        probs = (scores * weight).astype(BF16)
        h_res[:, cols] = dot(probs, v_ref[:, cols])
        return 0

    lax.fori_loop(0, heads, intra_head, 0)

    @pl.when(chip > 0)
    def _():
        state_copy(1).wait_recv()

    @pl.when((core == 1) & (chip > 0) & (chip < seqs // 2 - 1))
    def _():
        def add_state(h, _):
            decay = jnp.exp(logs[pl.ds(h, 1), :] + logs_before[pl.ds(h, 1), :])
            state_out[h] = (decay * state_in[h].astype(F32) + contrib[h]).astype(BF16)
            return 0

        lax.fori_loop(0, heads, add_state, 0)
        for step in (1, 2):
            state_copy(step).start()

    @pl.when((core == 0) & (chip == 0))
    def _():
        carried[...] = jnp.zeros_like(carried)

    @pl.when((core == 0) & (chip > 0))
    def _():
        carried[...] = state_in[...]

    @pl.when((core == 1) & (chip == 0))
    def _():
        carried[...] = pair_in[...]

    @pl.when((core == 1) & (chip > 0))
    def _():
        def join(h, _):
            carried[h] = (
                decay_row(logs_before, h) * state_in[h].astype(F32) + pair_in[h].astype(F32)
            ).astype(BF16)
            return 0

        lax.fori_loop(0, heads, join, 0)

    def inter_head(h, squares):
        c = head_cum(h)
        cols = head_lanes(h)
        raw = h_res[:, cols] + jnp.exp(c) * dot(q_ref[:, cols], carried[h])
        scale = lax.rsqrt(jnp.mean(raw * raw, axis=1, keepdims=True) + 1e-6)
        res = x_ref[:, cols].astype(F32) + raw * scale * attn_gain_ref[:, cols]
        h_res[:, cols] = res
        return squares + res * res

    squares = lax.fori_loop(0, heads, inter_head, jnp.zeros((block_len, dh), F32))
    scale = lax.rsqrt(jnp.sum(squares, axis=1, keepdims=True) * (1.0 / width) + 1e-6)

    def norm_head(h, _):
        cols = head_lanes(h)
        normed[:, cols] = (h_res[:, cols] * scale * norm_gain_ref[:, cols]).astype(BF16)
        return 0

    lax.fori_loop(0, heads, norm_head, 0)

    tile = 512

    def fill(to, e, at):
        def one(n, _):
            cols = pl.ds(pl.multiple_of(n * tile, tile), tile)
            to[at, :, cols] = dot(pick[e], normed[:, cols]).astype(BF16)
            return 0

        lax.fori_loop(0, width // tile, one, 0)

    def go_copy(peer, slot):
        return pltpu.make_async_remote_copy(
            send.at[peer],
            recv.at[slot],
            go_send_sem.at[peer],
            go_recv_sem.at[slot],
            {"exp": peer},
            MESH,
        )

    def back_copy(peer, slot):
        return pltpu.make_async_remote_copy(
            done.at[peer],
            back.at[slot],
            back_send_sem.at[peer],
            back_recv_sem.at[slot],
            {"exp": peer},
            MESH,
        )

    def dispatch(j, _):
        peer = flip(mine, owners - 1 - j, bits)
        fill(send, peer, peer)
        go_copy(peer, mine).start()
        return 0

    lax.fori_loop(0, owners - 1, dispatch, 0)
    fill(recv, mine, mine)
    for copy in weight_copies:
        copy.wait()

    def run_expert(source, to):
        def up(n, _):
            cols = pl.ds(pl.multiple_of(n * 256, 256), 256)
            gate_part = dot(recv[source], wg[:, cols])
            up_part = dot(recv[source], wu[:, cols])
            act[:, cols] = (gate_part / (1.0 + jnp.exp(-gate_part)) * up_part).astype(BF16)
            return 0

        lax.fori_loop(0, ff // 256, up, 0)

        def down_part(n, _):
            cols = pl.ds(pl.multiple_of(n * tile, tile), tile)
            to[source, :, cols] = dot(act[...], wd[:, cols]).astype(BF16)
            return 0

        lax.fori_loop(0, width // tile, down_part, 0)

    run_expert(mine, back)

    def serve(j, _):
        peer = flip(mine, owners - 1 - j, bits)
        go_copy(peer, peer).wait_recv()
        run_expert(peer, done)
        back_copy(peer, mine).start()
        return 0

    lax.fori_loop(0, owners - 1, serve, 0)

    def collect(j, _):
        peer = flip(mine, owners - 1 - j, bits)
        back_copy(peer, peer).wait_recv()
        return 0

    lax.fori_loop(0, owners - 1, collect, 0)

    def combine(n, _):
        cols = pl.ds(pl.multiple_of(n * tile, tile), tile)
        rows = back[:, :, cols].reshape(owners * cap, tile)
        out_ref[:, cols] = (h_res[:, cols] + dot(mix[...], rows)).astype(BF16)
        return 0

    lax.fori_loop(0, width // tile, combine, 0)

    def drain(j, _):
        peer = flip(mine, owners - 1 - j, bits)
        go_copy(peer, mine).wait_send()
        back_copy(peer, mine).wait_send()
        return 0

    lax.fori_loop(0, owners - 1, drain, 0)

    @pl.when(core == 0)
    def _():
        pair_copy(seq + 1).wait_send()
        log_copy(seq + 1).wait_send()

    @pl.when((core == 1) & (chip < seqs // 2 - 1))
    def _():
        for step in (1, 2):
            state_copy(step).wait_send()


def per_device(
    layer_input,
    queries,
    keys_in,
    values_in,
    decay_rate,
    attn_gain,
    norm_gain,
    expert_ids,
    gate_levels,
    w_gate,
    w_up,
    w_down,
):
    block_len, width = layer_input.shape[1:]
    heads = decay_rate.shape[2]
    dh = width // heads
    top = expert_ids.shape[2]
    ff = w_gate.shape[2]
    owners = lax.axis_size("exp")
    seqs = lax.axis_size("seq")
    cap = -(-(3 * block_len // owners) // 16) * 16
    vmem = pl.BlockSpec(memory_space=pltpu.VMEM)
    hbm = pl.BlockSpec(memory_space=pl.ANY)
    state = pltpu.VMEM((heads, dh, dh), BF16)
    rows = pltpu.VMEM((owners, cap, width), BF16)
    dma = pltpu.SemaphoreType.DMA
    out = pl.pallas_call(
        functools.partial(layer_kernel, (owners, cap, seqs, heads, top)),
        out_shape=jax.ShapeDtypeStruct((block_len, width), BF16),
        in_specs=[vmem] * 9 + [hbm] * 3,
        out_specs=vmem,
        scratch_shapes=[
            pltpu.VMEM((width, ff), BF16),
            pltpu.VMEM((width, ff), BF16),
            pltpu.VMEM((ff, width), BF16),
            pltpu.VMEM((block_len, heads), F32),
            pltpu.VMEM((heads, block_len), F32),
            pltpu.VMEM((heads, dh), F32),
            pltpu.VMEM((heads, dh), F32),
            pltpu.VMEM((heads, dh, dh), F32),
            state,
            state,
            state,
            state,
            pltpu.VMEM((block_len, width), F32),
            pltpu.VMEM((block_len, width), BF16),
            pltpu.VMEM((owners, cap, block_len), BF16),
            pltpu.VMEM((block_len, owners * cap), BF16),
            rows,
            rows,
            pltpu.VMEM((cap, ff), BF16),
            rows,
            rows,
            dma((3,)),
            dma((2,)),
            dma((2,)),
            dma((2,)),
            dma,
            dma((owners,)),
            dma((owners,)),
            dma((owners,)),
            dma((owners,)),
        ],
        compiler_params=pltpu.CompilerParams(
            collective_id=0, has_side_effects=True, vmem_limit_bytes=56 * 1024 * 1024
        ),
    )(
        layer_input[0],
        queries[0],
        keys_in[0],
        values_in[0],
        decay_rate[0],
        attn_gain[None],
        norm_gain[None],
        expert_ids[0],
        gate_levels[0],
        w_gate[0],
        w_up[0],
        w_down[0],
    )
    return out[None]


def solution(mesh):
    tokens = P("exp", "seq", None)
    experts = P("exp", None, None)
    return jax.shard_map(
        per_device,
        mesh=mesh,
        in_specs=(tokens,) * 5 + (P(), P()) + (tokens,) * 2 + (experts,) * 3,
        out_specs=tokens,
        check_vma=False,
    )
```

```python
import functools

import jax
import jax.numpy as jnp
from jax import lax
from jax.experimental import pallas as pl
from jax.experimental.pallas import tpu as pltpu
from jax.sharding import PartitionSpec as P

MESH = pl.DeviceIdType.MESH
F32 = jnp.float32
BF16 = jnp.bfloat16
PARTS = 4
UNROLL = 2


def flip(index, mask, bits):
    result = 0
    for b in range(bits):
        p = 1 << b
        result = result + p * lax.rem(lax.div(index, p) + lax.div(mask, p), 2)
    return result


def dot(a, b, contract=((1,), (0,)), **kw):
    return lax.dot_general(a, b, (contract, ((), ())), preferred_element_type=F32, **kw)


def layer_kernel(
    dims,
    x_ref,
    q_ref,
    k_ref,
    v_ref,
    decay_ref,
    attn_gain_ref,
    norm_gain_ref,
    ids_ref,
    levels_ref,
    wg_hbm,
    wu_hbm,
    wd_hbm,
    out_ref,
    wg,
    wu,
    wd,
    cum,
    cum_rows,
    logs,
    logs_before,
    contrib,
    state_out,
    pair_in,
    state_in,
    carried,
    h_res,
    normed,
    relay,
    info,
    info_in,
    pick,
    mix,
    send,
    recv,
    act,
    done,
    back,
    part_out,
    part_in,
    weight_sem,
    pair_sem,
    log_sem,
    state_send_sem,
    state_recv_sem,
    info_sem,
    relay_send_sem,
    relay_recv_sem,
    go_send_sem,
    go_recv_sem,
    back_send_sem,
    back_recv_sem,
    part_send_sem,
    part_recv_sem,
):
    owners, cap, seqs, heads, top = dims
    block_len, width = x_ref.shape
    dh = width // heads
    ff = wg.shape[1]
    half = owners // 2
    bits = half.bit_length() - 1
    parts, _, tile = normed.shape
    seq = lax.axis_index("seq")
    mine = lax.axis_index("exp")
    chip = lax.div(seq, 2)
    core = lax.rem(seq, 2)
    place = lax.rem(mine, half)
    base = mine - place
    partner = lax.rem(mine + half, owners)

    weight_copies = [
        pltpu.make_async_copy(hbm, vmem, weight_sem.at[i])
        for i, (hbm, vmem) in enumerate(((wg_hbm, wg), (wu_hbm, wu), (wd_hbm, wd)))
    ]
    for copy in weight_copies:
        copy.start()

    barrier = pltpu.get_barrier_semaphore()
    for step in range(1, seqs):
        pl.semaphore_signal(
            barrier, inc=1, device_id={"seq": lax.rem(seq + step, seqs)}, device_id_type=MESH
        )
    for step in range(1, half):
        pl.semaphore_signal(
            barrier,
            inc=1,
            device_id={"exp": base + lax.rem(place + step, half)},
            device_id_type=MESH,
        )
    pl.semaphore_signal(barrier, inc=1, device_id={"exp": partner}, device_id_type=MESH)

    down = lax.broadcasted_iota(jnp.int32, (block_len, block_len), 0)
    across = lax.broadcasted_iota(jnp.int32, (block_len, block_len), 1)
    lower = (down >= across).astype(F32)
    upper = (down <= across).astype(F32)
    rate = -decay_ref[...]
    cum[...] = dot(lower, rate, ((1,), (1,)), precision=lax.Precision.HIGHEST)
    cum_rows[...] = dot(rate, upper, precision=lax.Precision.HIGHEST)
    logs[...] = jnp.broadcast_to(cum_rows[:, block_len - 1 : block_len], logs.shape)
    lanes = lax.broadcasted_iota(jnp.int32, (block_len, heads), 1)

    def head_cum(h):
        return jnp.sum(jnp.where(lanes == h, cum[...], 0.0), axis=1, keepdims=True)

    def head_lanes(h):
        return pl.ds(pl.multiple_of(h * dh, dh), dh)

    def contrib_head(h, _):
        c = head_cum(h)
        cols = head_lanes(h)
        weight = jnp.exp(c[block_len - 1 :, :] - c)
        weighted = (k_ref[:, cols].astype(F32) * weight).astype(BF16)
        value = dot(weighted, v_ref[:, cols], ((0,), (0,)))
        contrib[h] = value
        state_out[h] = value.astype(BF16)
        return 0

    lax.fori_loop(0, heads, contrib_head, 0, unroll=UNROLL)
    pl.semaphore_wait(barrier, seqs - 1 + half)

    def pair_copy(target):
        return pltpu.make_async_remote_copy(
            state_out, pair_in, pair_sem.at[0], pair_sem.at[1], {"seq": target}, MESH
        )

    def log_copy(target):
        return pltpu.make_async_remote_copy(
            logs, logs_before, log_sem.at[0], log_sem.at[1], {"seq": target}, MESH
        )

    def state_copy(step):
        return pltpu.make_async_remote_copy(
            state_out,
            state_in,
            state_send_sem.at[step - 1],
            state_recv_sem,
            {"seq": lax.rem(seq + step, seqs)},
            MESH,
        )

    @pl.when(core == 0)
    def _():
        pair_copy(seq + 1).start()
        log_copy(seq + 1).start()

    expert = lax.broadcasted_iota(jnp.int32, (owners, block_len), 0)
    named = [(ids_ref[i : i + 1, :] == expert).astype(F32) for i in range(top)]
    member = sum(named)
    after = (down < across).astype(BF16)
    rank = dot(member.astype(BF16), after)
    info[0] = jnp.where(member > 0.5, rank, -1.0)
    info[1] = sum(
        named[i] * (levels_ref[i : i + 1, :].astype(F32) * (1.0 / 256.0)) for i in range(top)
    )
    info_copy = pltpu.make_async_remote_copy(
        info, info_in, info_sem.at[0], info_sem.at[1], {"exp": partner}, MESH
    )
    info_copy.start()

    def decay_row(ref, h):
        return jnp.exp(ref[pl.ds(h, 1), :])

    @pl.when(core == 1)
    def _():
        pair_copy(seq).wait_recv()
        log_copy(seq).wait_recv()

        def add_pair(h, _):
            both = decay_row(logs, h) * pair_in[h].astype(F32) + contrib[h]
            contrib[h] = both
            state_out[h] = both.astype(BF16)
            return 0

        lax.fori_loop(0, heads, add_pair, 0)

        @pl.when((chip == 0) & (seqs > 2))
        def _():
            for step in (1, 2):
                state_copy(step).start()

    def intra_head(h, _):
        c = head_cum(h)
        cols = head_lanes(h)
        scores = dot(q_ref[:, cols], k_ref[:, cols], ((1,), (1,)))
        gap = c - cum_rows[pl.ds(h, 1), :]
        weight = jnp.where(down >= across, jnp.exp(jnp.minimum(gap, 0.0)), 0.0)
        probs = (scores * weight).astype(BF16)
        h_res[:, cols] = dot(probs, v_ref[:, cols])
        return 0

    lax.fori_loop(0, heads, intra_head, 0, unroll=UNROLL)

    slot = lax.broadcasted_iota(jnp.int32, (cap, block_len), 0).astype(F32)
    same = (down == across).astype(BF16)

    def slots(group, source):
        spread = []
        for n in range(half):
            hit = source[0, pl.ds(base + n, 1), :] == slot
            pick[group, n] = jnp.where(hit, 1.0, 0.0).astype(BF16)
            spread.append(jnp.where(hit, source[1, pl.ds(base + n, 1), :], 0.0).astype(BF16))
        mix[group] = dot(same, jnp.concatenate(spread, axis=0), ((1,), (1,))).astype(BF16)

    slots(0, info)
    info_copy.wait_recv()
    slots(1, info_in)

    @pl.when(chip > 0)
    def _():
        state_copy(1).wait_recv()

    @pl.when((core == 1) & (chip > 0) & (chip < seqs // 2 - 1))
    def _():
        def add_state(h, _):
            decay = jnp.exp(logs[pl.ds(h, 1), :] + logs_before[pl.ds(h, 1), :])
            state_out[h] = (decay * state_in[h].astype(F32) + contrib[h]).astype(BF16)
            return 0

        lax.fori_loop(0, heads, add_state, 0)
        for step in (1, 2):
            state_copy(step).start()

    @pl.when((core == 0) & (chip == 0))
    def _():
        carried[...] = jnp.zeros_like(carried)

    @pl.when((core == 0) & (chip > 0))
    def _():
        carried[...] = state_in[...]

    @pl.when((core == 1) & (chip == 0))
    def _():
        carried[...] = pair_in[...]

    @pl.when((core == 1) & (chip > 0))
    def _():
        def join(h, _):
            carried[h] = (
                decay_row(logs_before, h) * state_in[h].astype(F32) + pair_in[h].astype(F32)
            ).astype(BF16)
            return 0

        lax.fori_loop(0, heads, join, 0)

    def inter_head(h, squares):
        c = head_cum(h)
        cols = head_lanes(h)
        raw = h_res[:, cols] + jnp.exp(c) * dot(q_ref[:, cols], carried[h])
        scale = lax.rsqrt(jnp.mean(raw * raw, axis=1, keepdims=True) + 1e-6)
        res = x_ref[:, cols].astype(F32) + raw * scale * attn_gain_ref[:, cols]
        h_res[:, cols] = res
        return squares + res * res

    squares = lax.fori_loop(
        0, heads, inter_head, jnp.zeros((block_len, dh), F32), unroll=UNROLL
    )
    scale = lax.rsqrt(jnp.sum(squares, axis=1, keepdims=True) * (1.0 / width) + 1e-6)

    def part_cols(c):
        return pl.ds(c * tile, tile)

    def relay_copy(c):
        return pltpu.make_async_remote_copy(
            normed.at[c],
            relay.at[c],
            relay_send_sem.at[c],
            relay_recv_sem.at[c],
            {"exp": partner},
            MESH,
        )

    def part_copy(c):
        return pltpu.make_async_remote_copy(
            part_out.at[c],
            part_in.at[c],
            part_send_sem.at[c],
            part_recv_sem.at[c],
            {"exp": partner},
            MESH,
        )

    def near_copy(source, target, send_sem, recv_sem, group, c, peer, slot):
        if group == 0:
            source, target = source.at[0, peer], target.at[0, slot]
        else:
            source, target = source.at[1, peer, c], target.at[1, slot, c]
        return pltpu.make_async_remote_copy(
            source,
            target,
            send_sem.at[group, peer, c],
            recv_sem.at[group, slot, c],
            {"exp": base + peer},
            MESH,
        )

    def go_copy(group, c, peer, slot):
        return near_copy(send, recv, go_send_sem, go_recv_sem, group, c, peer, slot)

    def back_copy(group, c, peer, slot):
        return near_copy(done, back, back_send_sem, back_recv_sem, group, c, peer, slot)

    def each_peer(action):
        def one(j, _):
            action(flip(place, half - 1 - j, bits))
            return 0

        lax.fori_loop(0, half - 1, one, 0)

    def fill(group, c, source):
        rows = dot(pick[group].reshape(half * cap, block_len), source[c])
        send[group, :, c] = rows.astype(BF16).reshape(half, cap, tile)
        recv[group, place, c] = send[group, place, c]

    def run_up(group):
        def one(n, _):
            cols = pl.ds(pl.multiple_of(n * 256, 256), 256)
            gate_part = up_part = 0.0
            for c in range(parts):
                rows = recv[group, :, c].reshape(half * cap, tile)
                gate_part = gate_part + dot(rows, wg[part_cols(c), cols])
                up_part = up_part + dot(rows, wu[part_cols(c), cols])
            act[:, cols] = (gate_part / (1.0 + jnp.exp(-gate_part)) * up_part).astype(BF16)
            return 0

        lax.fori_loop(0, ff // 256, one, 0)

    def run_down(group, c):
        rows = dot(act[...], wd[:, part_cols(c)]).astype(BF16)
        done[group, :, c] = rows.reshape(half, cap, tile)
        back[group, place, c] = done[group, place, c]

    for c in range(parts):
        normed[c] = (h_res[:, part_cols(c)] * scale * norm_gain_ref[:, part_cols(c)]).astype(BF16)
        relay_copy(c).start()
    for c in range(parts):
        fill(0, c, normed)
    each_peer(lambda peer: go_copy(0, 0, peer, place).start())
    for copy in weight_copies:
        copy.wait()

    for c in range(parts):
        if c == parts - 1:
            each_peer(lambda peer: go_copy(0, 0, peer, peer).wait_recv())
            run_up(0)
            for d in range(parts):
                run_down(0, d)
            each_peer(lambda peer: back_copy(0, 0, peer, place).start())
        relay_copy(c).wait_recv()
        fill(1, c, relay)
        each_peer(lambda peer, c=c: go_copy(1, c, peer, place).start())

    for c in range(parts):
        each_peer(lambda peer, c=c: go_copy(1, c, peer, peer).wait_recv())
    run_up(1)
    for c in range(parts):
        run_down(1, c)
        each_peer(lambda peer, c=c: back_copy(1, c, peer, place).start())

    def mixed(group, c):
        return dot(mix[group], back[group, :, c].reshape(half * cap, tile))

    for c in range(parts):
        each_peer(lambda peer, c=c: back_copy(1, c, peer, peer).wait_recv())
        part_out[c] = mixed(1, c).astype(BF16)
        part_copy(c).start()

    each_peer(lambda peer: back_copy(0, 0, peer, peer).wait_recv())
    for c in range(parts):
        h_res[:, part_cols(c)] += mixed(0, c)
    for c in range(parts):
        part_copy(c).wait_recv()
        out_ref[:, part_cols(c)] = (h_res[:, part_cols(c)] + part_in[c].astype(F32)).astype(BF16)

    info_copy.wait_send()
    for c in range(parts):
        relay_copy(c).wait_send()
        part_copy(c).wait_send()
        each_peer(lambda peer, c=c: go_copy(1, c, peer, place).wait_send())
        each_peer(lambda peer, c=c: back_copy(1, c, peer, place).wait_send())
    each_peer(lambda peer: go_copy(0, 0, peer, place).wait_send())
    each_peer(lambda peer: back_copy(0, 0, peer, place).wait_send())

    @pl.when(core == 0)
    def _():
        pair_copy(seq + 1).wait_send()
        log_copy(seq + 1).wait_send()

    @pl.when((core == 1) & (chip < seqs // 2 - 1))
    def _():
        for step in (1, 2):
            state_copy(step).wait_send()


def per_device(
    layer_input,
    queries,
    keys_in,
    values_in,
    decay_rate,
    attn_gain,
    norm_gain,
    expert_ids,
    gate_levels,
    w_gate,
    w_up,
    w_down,
):
    block_len, width = layer_input.shape[1:]
    heads = decay_rate.shape[2]
    dh = width // heads
    top = expert_ids.shape[2]
    ff = w_gate.shape[2]
    owners = lax.axis_size("exp")
    seqs = lax.axis_size("seq")
    half = owners // 2
    cap = -(-(3 * block_len // owners) // 16) * 16
    tile = width // PARTS
    vmem = pl.BlockSpec(memory_space=pltpu.VMEM)
    hbm = pl.BlockSpec(memory_space=pl.ANY)
    state = pltpu.VMEM((heads, dh, dh), BF16)
    rows = pltpu.VMEM((2, half, PARTS, cap, tile), BF16)
    columns = pltpu.VMEM((PARTS, block_len, tile), BF16)
    known = pltpu.VMEM((2, owners, block_len), F32)
    dma = pltpu.SemaphoreType.DMA
    near = dma((2, half, PARTS))
    out = pl.pallas_call(
        functools.partial(layer_kernel, (owners, cap, seqs, heads, top)),
        out_shape=jax.ShapeDtypeStruct((block_len, width), BF16),
        in_specs=[vmem] * 9 + [hbm] * 3,
        out_specs=vmem,
        scratch_shapes=[
            pltpu.VMEM((width, ff), BF16),
            pltpu.VMEM((width, ff), BF16),
            pltpu.VMEM((ff, width), BF16),
            pltpu.VMEM((block_len, heads), F32),
            pltpu.VMEM((heads, block_len), F32),
            pltpu.VMEM((heads, dh), F32),
            pltpu.VMEM((heads, dh), F32),
            pltpu.VMEM((heads, dh, dh), F32),
            state,
            state,
            state,
            state,
            pltpu.VMEM((block_len, width), F32),
            columns,
            columns,
            known,
            known,
            pltpu.VMEM((2, half, cap, block_len), BF16),
            pltpu.VMEM((2, block_len, half * cap), BF16),
            rows,
            rows,
            pltpu.VMEM((half * cap, ff), BF16),
            rows,
            rows,
            columns,
            columns,
            dma((3,)),
            dma((2,)),
            dma((2,)),
            dma((2,)),
            dma,
            dma((2,)),
            dma((PARTS,)),
            dma((PARTS,)),
            near,
            near,
            near,
            near,
            dma((PARTS,)),
            dma((PARTS,)),
        ],
        compiler_params=pltpu.CompilerParams(
            collective_id=0, has_side_effects=True, vmem_limit_bytes=56 * 1024 * 1024
        ),
    )(
        layer_input[0],
        queries[0],
        keys_in[0],
        values_in[0],
        decay_rate[0].T,
        attn_gain[None],
        norm_gain[None],
        expert_ids[0].T,
        gate_levels[0].T,
        w_gate[0],
        w_up[0],
        w_down[0],
    )
    return out[None]


def solution(mesh):
    tokens = P("exp", "seq", None)
    experts = P("exp", None, None)
    return jax.shard_map(
        per_device,
        mesh=mesh,
        in_specs=(tokens,) * 5 + (P(), P()) + (tokens,) * 2 + (experts,) * 3,
        out_specs=tokens,
        check_vma=False,
    )
```

```python
import functools

import jax
import jax.numpy as jnp
from jax import lax
from jax.experimental import pallas as pl
from jax.experimental.pallas import tpu as pltpu
from jax.sharding import PartitionSpec as P

MESH = pl.DeviceIdType.MESH
F32 = jnp.float32
BF16 = jnp.bfloat16
PARTS = 4
GROUPS = 4


def flip(index, mask, bits):
    result = 0
    for b in range(bits):
        p = 1 << b
        result = result + p * lax.rem(lax.div(index, p) + lax.div(mask, p), 2)
    return result


def dot(a, b, contract=((1,), (0,)), **kw):
    return lax.dot_general(a, b, (contract, ((), ())), preferred_element_type=F32, **kw)


def layer_kernel(
    dims,
    x_ref,
    q_ref,
    k_ref,
    v_ref,
    decay_ref,
    attn_gain_ref,
    norm_gain_ref,
    ids_ref,
    levels_ref,
    wg_hbm,
    wu_hbm,
    wd_hbm,
    out_ref,
    wg,
    wu,
    wd,
    cum,
    cum_rows,
    logs,
    logs_before,
    contrib,
    state_out,
    pair_in,
    state_in,
    carried,
    h_res,
    normed,
    relay,
    info,
    info_in,
    pick,
    mix,
    send,
    recv,
    act,
    done,
    back,
    part_out,
    part_in,
    weight_sem,
    pair_sem,
    log_sem,
    state_send_sem,
    state_recv_sem,
    info_sem,
    relay_send_sem,
    relay_recv_sem,
    go_send_sem,
    go_recv_sem,
    back_send_sem,
    back_recv_sem,
    part_send_sem,
    part_recv_sem,
):
    owners, cap, seqs, heads, top = dims
    block_len, width = x_ref.shape
    dh = width // heads
    ff = wg.shape[1]
    half = owners // 2
    bits = half.bit_length() - 1
    parts, _, tile = normed.shape
    seq = lax.axis_index("seq")
    mine = lax.axis_index("exp")
    chip = lax.div(seq, 2)
    core = lax.rem(seq, 2)
    place = lax.rem(mine, half)
    base = mine - place
    partner = lax.rem(mine + half, owners)

    weight_copies = [
        pltpu.make_async_copy(hbm, vmem, weight_sem.at[i])
        for i, (hbm, vmem) in enumerate(((wg_hbm, wg), (wu_hbm, wu), (wd_hbm, wd)))
    ]
    for copy in weight_copies:
        copy.start()

    barrier = pltpu.get_barrier_semaphore()
    for step in range(1, seqs):
        pl.semaphore_signal(
            barrier, inc=1, device_id={"seq": lax.rem(seq + step, seqs)}, device_id_type=MESH
        )
    for step in range(1, half):
        pl.semaphore_signal(
            barrier,
            inc=1,
            device_id={"exp": base + lax.rem(place + step, half)},
            device_id_type=MESH,
        )
    pl.semaphore_signal(barrier, inc=1, device_id={"exp": partner}, device_id_type=MESH)

    down = lax.broadcasted_iota(jnp.int32, (block_len, block_len), 0)
    across = lax.broadcasted_iota(jnp.int32, (block_len, block_len), 1)
    lower = (down >= across).astype(F32)
    upper = (down <= across).astype(F32)
    rate = -decay_ref[...]
    cum[...] = dot(lower, rate, ((1,), (1,)), precision=lax.Precision.HIGHEST)
    cum_rows[...] = dot(rate, upper, precision=lax.Precision.HIGHEST)
    logs[...] = jnp.broadcast_to(cum_rows[:, block_len - 1 : block_len], logs.shape)
    lanes = lax.broadcasted_iota(jnp.int32, (block_len, heads), 1)

    def head_cum(h):
        return jnp.sum(jnp.where(lanes == h, cum[...], 0.0), axis=1, keepdims=True)

    def head_lanes(h):
        return pl.ds(pl.multiple_of(h * dh, dh), dh)

    def contrib_head(h, _):
        c = head_cum(h)
        cols = head_lanes(h)
        weight = jnp.exp(c[block_len - 1 :, :] - c)
        weighted = (k_ref[:, cols].astype(F32) * weight).astype(BF16)
        value = dot(weighted, v_ref[:, cols], ((0,), (0,)))
        contrib[h] = value
        state_out[h] = value.astype(BF16)
        return 0

    per_group = heads // GROUPS

    def group(ref, g):
        return ref.at[pl.ds(g * per_group, per_group)]

    def each_head(g, body, start=0):
        return lax.fori_loop(g * per_group, (g + 1) * per_group, body, start, unroll=per_group)

    def pair_copy(target, g):
        return pltpu.make_async_remote_copy(
            group(state_out, g),
            group(pair_in, g),
            pair_sem.at[0, g],
            pair_sem.at[1, g],
            {"seq": target},
            MESH,
        )

    def log_copy(target):
        return pltpu.make_async_remote_copy(
            logs, logs_before, log_sem.at[0], log_sem.at[1], {"seq": target}, MESH
        )

    def state_copy(step, g):
        return pltpu.make_async_remote_copy(
            group(state_out, g),
            group(state_in, g),
            state_send_sem.at[step - 1, g],
            state_recv_sem.at[g],
            {"seq": lax.rem(seq + step, seqs)},
            MESH,
        )

    def decay_row(ref, h):
        return jnp.exp(ref[pl.ds(h, 1), :])

    def add_pair(h, _):
        both = decay_row(logs, h) * pair_in[h].astype(F32) + contrib[h]
        contrib[h] = both
        state_out[h] = both.astype(BF16)
        return 0

    for g in range(GROUPS + 1):
        if g < GROUPS:
            each_head(g, contrib_head)
        if g == 0:
            pl.semaphore_wait(barrier, seqs - 1 + half)

            @pl.when(core == 0)
            def _():
                log_copy(seq + 1).start()

        if g < GROUPS:

            @pl.when(core == 0)
            def _(g=g):
                pair_copy(seq + 1, g).start()

        if g > 0:

            @pl.when(core == 1)
            def _(g=g - 1):
                if g == 0:
                    log_copy(seq).wait_recv()
                pair_copy(seq, g).wait_recv()
                each_head(g, add_pair)

                @pl.when((chip == 0) & (seqs > 2))
                def _():
                    for step in (1, 2):
                        state_copy(step, g).start()

    expert = lax.broadcasted_iota(jnp.int32, (owners, block_len), 0)
    named = [(ids_ref[i : i + 1, :] == expert).astype(F32) for i in range(top)]
    member = sum(named)
    after = (down < across).astype(BF16)
    rank = dot(member.astype(BF16), after)
    info[0] = jnp.where(member > 0.5, rank, -1.0)
    info[1] = sum(
        named[i] * (levels_ref[i : i + 1, :].astype(F32) * (1.0 / 256.0)) for i in range(top)
    )
    info_copy = pltpu.make_async_remote_copy(
        info, info_in, info_sem.at[0], info_sem.at[1], {"exp": partner}, MESH
    )
    info_copy.start()

    def intra_head(h, _):
        c = head_cum(h)
        cols = head_lanes(h)
        scores = dot(q_ref[:, cols], k_ref[:, cols], ((1,), (1,)))
        gap = c - cum_rows[pl.ds(h, 1), :]
        weight = jnp.where(down >= across, jnp.exp(jnp.minimum(gap, 0.0)), 0.0)
        probs = (scores * weight).astype(BF16)
        h_res[:, cols] = dot(probs, v_ref[:, cols])
        return 0

    lax.fori_loop(0, heads, intra_head, 0, unroll=per_group)

    slot = lax.broadcasted_iota(jnp.int32, (cap, block_len), 0).astype(F32)
    same = (down == across).astype(BF16)

    def slots(group, source):
        spread = []
        for n in range(half):
            hit = source[0, pl.ds(base + n, 1), :] == slot
            pick[group, n] = jnp.where(hit, 1.0, 0.0).astype(BF16)
            spread.append(jnp.where(hit, source[1, pl.ds(base + n, 1), :], 0.0).astype(BF16))
        mix[group] = dot(same, jnp.concatenate(spread, axis=0), ((1,), (1,))).astype(BF16)

    slots(0, info)
    info_copy.wait_recv()
    slots(1, info_in)

    def add_state(h, _):
        decay = jnp.exp(logs[pl.ds(h, 1), :] + logs_before[pl.ds(h, 1), :])
        state_out[h] = (decay * state_in[h].astype(F32) + contrib[h]).astype(BF16)
        return 0

    def join(h, _):
        carried[h] = (
            decay_row(logs_before, h) * state_in[h].astype(F32) + pair_in[h].astype(F32)
        ).astype(BF16)
        return 0

    def carry(g):
        to, before, passed = group(carried, g), group(pair_in, g), group(state_in, g)

        @pl.when(chip > 0)
        def _():
            state_copy(1, g).wait_recv()

        @pl.when((core == 1) & (chip > 0) & (chip < seqs // 2 - 1))
        def _():
            each_head(g, add_state)
            for step in (1, 2):
                state_copy(step, g).start()

        @pl.when((core == 0) & (chip == 0))
        def _():
            to[...] = jnp.zeros_like(to)

        @pl.when((core == 0) & (chip > 0))
        def _():
            to[...] = passed[...]

        @pl.when((core == 1) & (chip == 0))
        def _():
            to[...] = before[...]

        @pl.when((core == 1) & (chip > 0))
        def _():
            each_head(g, join)

    def inter_head(h, squares):
        c = head_cum(h)
        cols = head_lanes(h)
        raw = h_res[:, cols] + jnp.exp(c) * dot(q_ref[:, cols], carried[h])
        scale = lax.rsqrt(jnp.mean(raw * raw, axis=1, keepdims=True) + 1e-6)
        res = x_ref[:, cols].astype(F32) + raw * scale * attn_gain_ref[:, cols]
        h_res[:, cols] = res
        return squares + res * res

    squares = jnp.zeros((block_len, dh), F32)
    for g in range(GROUPS):
        carry(g)
        squares = each_head(g, inter_head, squares)
    scale = lax.rsqrt(jnp.sum(squares, axis=1, keepdims=True) * (1.0 / width) + 1e-6)

    def part_cols(c):
        return pl.ds(c * tile, tile)

    def relay_copy(c):
        return pltpu.make_async_remote_copy(
            normed.at[c],
            relay.at[c],
            relay_send_sem.at[c],
            relay_recv_sem.at[c],
            {"exp": partner},
            MESH,
        )

    def part_copy(c):
        return pltpu.make_async_remote_copy(
            part_out.at[c],
            part_in.at[c],
            part_send_sem.at[c],
            part_recv_sem.at[c],
            {"exp": partner},
            MESH,
        )

    def near_copy(source, target, send_sem, recv_sem, group, c, peer, slot):
        if group == 0:
            source, target = source.at[0, peer], target.at[0, slot]
        else:
            source, target = source.at[1, peer, c], target.at[1, slot, c]
        return pltpu.make_async_remote_copy(
            source,
            target,
            send_sem.at[group, peer, c],
            recv_sem.at[group, slot, c],
            {"exp": base + peer},
            MESH,
        )

    def go_copy(group, c, peer, slot):
        return near_copy(send, recv, go_send_sem, go_recv_sem, group, c, peer, slot)

    def back_copy(group, c, peer, slot):
        return near_copy(done, back, back_send_sem, back_recv_sem, group, c, peer, slot)

    def each_peer(action):
        def one(j, _):
            action(flip(place, half - 1 - j, bits))
            return 0

        lax.fori_loop(0, half - 1, one, 0)

    def fill(group, c, source):
        rows = dot(pick[group].reshape(half * cap, block_len), source[c])
        send[group, :, c] = rows.astype(BF16).reshape(half, cap, tile)
        recv[group, place, c] = send[group, place, c]

    def run_up(group):
        def one(n, _):
            cols = pl.ds(pl.multiple_of(n * 256, 256), 256)
            gate_part = up_part = 0.0
            for c in range(parts):
                rows = recv[group, :, c].reshape(half * cap, tile)
                gate_part = gate_part + dot(rows, wg[part_cols(c), cols])
                up_part = up_part + dot(rows, wu[part_cols(c), cols])
            act[group, :, cols] = (gate_part / (1.0 + jnp.exp(-gate_part)) * up_part).astype(BF16)
            return 0

        lax.fori_loop(0, ff // 256, one, 0)

    def run_down(group, c):
        rows = dot(act[group], wd[:, part_cols(c)]).astype(BF16)
        done[group, :, c] = rows.reshape(half, cap, tile)
        back[group, place, c] = done[group, place, c]

    for c in range(parts):
        normed[c] = (h_res[:, part_cols(c)] * scale * norm_gain_ref[:, part_cols(c)]).astype(BF16)
        relay_copy(c).start()
    for c in range(parts):
        fill(0, c, normed)
    each_peer(lambda peer: go_copy(0, 0, peer, place).start())
    for copy in weight_copies:
        copy.wait()

    for c in range(parts):
        if c == parts - 1:
            each_peer(lambda peer: go_copy(0, 0, peer, peer).wait_recv())
            run_up(0)
        relay_copy(c).wait_recv()
        fill(1, c, relay)
        each_peer(lambda peer, c=c: go_copy(1, c, peer, place).start())

    for c in range(parts):
        each_peer(lambda peer, c=c: go_copy(1, c, peer, peer).wait_recv())
    run_up(1)
    for c in range(parts):
        run_down(1, c)
        each_peer(lambda peer, c=c: back_copy(1, c, peer, place).start())
    for c in range(parts):
        run_down(0, c)
    each_peer(lambda peer: back_copy(0, 0, peer, place).start())

    def mixed(group, c):
        return dot(mix[group], back[group, :, c].reshape(half * cap, tile))

    for c in range(parts):
        each_peer(lambda peer, c=c: back_copy(1, c, peer, peer).wait_recv())
        part_out[c] = mixed(1, c).astype(BF16)
        part_copy(c).start()

    each_peer(lambda peer: back_copy(0, 0, peer, peer).wait_recv())
    for c in range(parts):
        h_res[:, part_cols(c)] += mixed(0, c)
    for c in range(parts):
        part_copy(c).wait_recv()
        out_ref[:, part_cols(c)] = (h_res[:, part_cols(c)] + part_in[c].astype(F32)).astype(BF16)

    info_copy.wait_send()
    for c in range(parts):
        relay_copy(c).wait_send()
        part_copy(c).wait_send()
        each_peer(lambda peer, c=c: go_copy(1, c, peer, place).wait_send())
        each_peer(lambda peer, c=c: back_copy(1, c, peer, place).wait_send())
    each_peer(lambda peer: go_copy(0, 0, peer, place).wait_send())
    each_peer(lambda peer: back_copy(0, 0, peer, place).wait_send())

    @pl.when(core == 0)
    def _():
        log_copy(seq + 1).wait_send()
        for g in range(GROUPS):
            pair_copy(seq + 1, g).wait_send()

    @pl.when((core == 1) & (chip < seqs // 2 - 1))
    def _():
        for g in range(GROUPS):
            for step in (1, 2):
                state_copy(step, g).wait_send()


def per_device(
    layer_input,
    queries,
    keys_in,
    values_in,
    decay_rate,
    attn_gain,
    norm_gain,
    expert_ids,
    gate_levels,
    w_gate,
    w_up,
    w_down,
):
    block_len, width = layer_input.shape[1:]
    heads = decay_rate.shape[2]
    dh = width // heads
    top = expert_ids.shape[2]
    ff = w_gate.shape[2]
    owners = lax.axis_size("exp")
    seqs = lax.axis_size("seq")
    half = owners // 2
    cap = -(-(3 * block_len // owners) // 16) * 16
    tile = width // PARTS
    vmem = pl.BlockSpec(memory_space=pltpu.VMEM)
    hbm = pl.BlockSpec(memory_space=pl.ANY)
    state = pltpu.VMEM((heads, dh, dh), BF16)
    rows = pltpu.VMEM((2, half, PARTS, cap, tile), BF16)
    columns = pltpu.VMEM((PARTS, block_len, tile), BF16)
    known = pltpu.VMEM((2, owners, block_len), F32)
    dma = pltpu.SemaphoreType.DMA
    near = dma((2, half, PARTS))
    out = pl.pallas_call(
        functools.partial(layer_kernel, (owners, cap, seqs, heads, top)),
        out_shape=jax.ShapeDtypeStruct((block_len, width), BF16),
        in_specs=[vmem] * 9 + [hbm] * 3,
        out_specs=vmem,
        scratch_shapes=[
            pltpu.VMEM((width, ff), BF16),
            pltpu.VMEM((width, ff), BF16),
            pltpu.VMEM((ff, width), BF16),
            pltpu.VMEM((block_len, heads), F32),
            pltpu.VMEM((heads, block_len), F32),
            pltpu.VMEM((heads, dh), F32),
            pltpu.VMEM((heads, dh), F32),
            pltpu.VMEM((heads, dh, dh), F32),
            state,
            state,
            state,
            state,
            pltpu.VMEM((block_len, width), F32),
            columns,
            columns,
            known,
            known,
            pltpu.VMEM((2, half, cap, block_len), BF16),
            pltpu.VMEM((2, block_len, half * cap), BF16),
            rows,
            rows,
            pltpu.VMEM((2, half * cap, ff), BF16),
            rows,
            rows,
            columns,
            columns,
            dma((3,)),
            dma((2, GROUPS)),
            dma((2,)),
            dma((2, GROUPS)),
            dma((GROUPS,)),
            dma((2,)),
            dma((PARTS,)),
            dma((PARTS,)),
            near,
            near,
            near,
            near,
            dma((PARTS,)),
            dma((PARTS,)),
        ],
        compiler_params=pltpu.CompilerParams(
            collective_id=0, has_side_effects=True, vmem_limit_bytes=56 * 1024 * 1024
        ),
    )(
        layer_input[0],
        queries[0],
        keys_in[0],
        values_in[0],
        decay_rate[0].T,
        attn_gain[None],
        norm_gain[None],
        expert_ids[0].T,
        gate_levels[0].T,
        w_gate[0],
        w_up[0],
        w_down[0],
    )
    return out[None]


def solution(mesh):
    tokens = P("exp", "seq", None)
    experts = P("exp", None, None)
    return jax.shard_map(
        per_device,
        mesh=mesh,
        in_specs=(tokens,) * 5 + (P(), P()) + (tokens,) * 2 + (experts,) * 3,
        out_specs=tokens,
        check_vma=False,
    )
```

```python
import functools

import jax
import jax.numpy as jnp
from jax import lax
from jax.experimental import pallas as pl
from jax.experimental.pallas import tpu as pltpu
from jax.sharding import PartitionSpec as P

MESH = pl.DeviceIdType.MESH
F32 = jnp.float32
BF16 = jnp.bfloat16
PARTS = 4
GROUPS = 4


def flip(index, mask, bits):
    result = 0
    for b in range(bits):
        p = 1 << b
        result = result + p * lax.rem(lax.div(index, p) + lax.div(mask, p), 2)
    return result


def dot(a, b, contract=((1,), (0,)), **kw):
    return lax.dot_general(a, b, (contract, ((), ())), preferred_element_type=F32, **kw)


def layer_kernel(
    dims,
    x_ref,
    q_ref,
    k_ref,
    v_ref,
    decay_ref,
    attn_gain_ref,
    norm_gain_ref,
    ids_ref,
    levels_ref,
    wg_hbm,
    wu_hbm,
    wd_hbm,
    out_ref,
    wg,
    wu,
    wd,
    cum,
    cum_rows,
    logs,
    logs_before,
    contrib,
    state_out,
    pair_in,
    state_in,
    carried,
    h_res,
    normed,
    relay,
    info,
    info_in,
    pick,
    mix,
    send,
    send_on,
    recv,
    act,
    done,
    back,
    back_on,
    part_out,
    part_in,
    weight_sem,
    pair_sem,
    log_sem,
    state_send_sem,
    state_recv_sem,
    state_pass_sem,
    info_send_sem,
    info_recv_sem,
    relay_send_sem,
    relay_recv_sem,
    go_send_sem,
    go_recv_sem,
    go_on_send_sem,
    go_on_recv_sem,
    back_send_sem,
    back_recv_sem,
    back_on_send_sem,
    back_on_recv_sem,
    part_send_sem,
    part_recv_sem,
):
    owners, cap, seqs, heads, top = dims
    block_len, width = x_ref.shape
    dh = width // heads
    ff = wg.shape[1]
    half = owners // 2
    bits = half.bit_length() - 1
    parts, _, tile = normed.shape
    seq = lax.axis_index("seq")
    mine = lax.axis_index("exp")
    chip = lax.div(seq, 2)
    core = lax.rem(seq, 2)
    place = lax.rem(mine, half)
    base = mine - place
    quarter = half // 2
    side = lax.div(mine, half)
    line = lax.div(place, quarter)
    low = lax.rem(place, quarter)
    proxy = side + line == 1
    target = (1 - side) * half + side * quarter + low

    def client(i):
        return (1 - side) * half + i * quarter + low

    def proxy_place(i):
        return (1 - side) * quarter + i

    weight_copies = [
        pltpu.make_async_copy(hbm, vmem, weight_sem.at[i])
        for i, (hbm, vmem) in enumerate(((wg_hbm, wg), (wu_hbm, wu), (wd_hbm, wd)))
    ]
    for copy in weight_copies:
        copy.start()

    barrier = pltpu.get_barrier_semaphore()
    for step in range(1, seqs):
        pl.semaphore_signal(
            barrier, inc=1, device_id={"seq": lax.rem(seq + step, seqs)}, device_id_type=MESH
        )
    for step in range(1, half):
        pl.semaphore_signal(
            barrier,
            inc=1,
            device_id={"exp": base + lax.rem(place + step, half)},
            device_id_type=MESH,
        )
    pl.semaphore_signal(barrier, inc=1, device_id={"exp": target}, device_id_type=MESH)

    @pl.when(proxy)
    def _():
        for i in range(2):
            pl.semaphore_signal(barrier, inc=1, device_id={"exp": client(i)}, device_id_type=MESH)


    down = lax.broadcasted_iota(jnp.int32, (block_len, block_len), 0)
    across = lax.broadcasted_iota(jnp.int32, (block_len, block_len), 1)
    lower = (down >= across).astype(F32)
    upper = (down <= across).astype(F32)
    rate = -decay_ref[...]
    cum[...] = dot(lower, rate, ((1,), (1,)), precision=lax.Precision.HIGHEST)
    cum_rows[...] = dot(rate, upper, precision=lax.Precision.HIGHEST)
    logs[...] = jnp.broadcast_to(cum_rows[:, block_len - 1 : block_len], logs.shape)
    lanes = lax.broadcasted_iota(jnp.int32, (block_len, heads), 1)

    def head_cum(h):
        return jnp.sum(jnp.where(lanes == h, cum[...], 0.0), axis=1, keepdims=True)

    def head_lanes(h):
        return pl.ds(pl.multiple_of(h * dh, dh), dh)

    def contrib_head(h, _):
        c = head_cum(h)
        cols = head_lanes(h)
        weight = jnp.exp(c[block_len - 1 :, :] - c)
        weighted = (k_ref[:, cols].astype(F32) * weight).astype(BF16)
        value = dot(weighted, v_ref[:, cols], ((0,), (0,)))
        contrib[h] = value
        state_out[h] = value.astype(BF16)
        return 0

    per_group = heads // GROUPS

    def group(ref, g):
        return ref.at[pl.ds(g * per_group, per_group)]

    def each_head(g, body, start=0):
        return lax.fori_loop(g * per_group, (g + 1) * per_group, body, start, unroll=per_group)

    def pair_copy(target, g):
        return pltpu.make_async_remote_copy(
            group(state_out, g),
            group(pair_in, g),
            pair_sem.at[0, g],
            pair_sem.at[1, g],
            {"seq": target},
            MESH,
        )

    def log_copy(target):
        return pltpu.make_async_remote_copy(
            logs, logs_before, log_sem.at[0], log_sem.at[1], {"seq": target}, MESH
        )

    def state_copy(g):
        return pltpu.make_async_remote_copy(
            group(state_out, g),
            group(state_in, g),
            state_send_sem.at[g],
            state_recv_sem.at[g],
            {"seq": lax.rem(seq + 1 + g % 2, seqs)},
            MESH,
        )

    def pass_copy(g):
        return pltpu.make_async_remote_copy(
            group(state_in, g),
            group(state_in, g),
            state_pass_sem.at[g],
            state_recv_sem.at[g],
            {"seq": seq + 1 - 2 * core},
            MESH,
        )

    def decay_row(ref, h):
        return jnp.exp(ref[pl.ds(h, 1), :])

    def add_pair(h, _):
        both = decay_row(logs, h) * pair_in[h].astype(F32) + contrib[h]
        contrib[h] = both
        state_out[h] = both.astype(BF16)
        return 0

    for g in range(GROUPS + 1):
        if g < GROUPS:
            each_head(g, contrib_head)
        if g == 0:

            @pl.when(proxy)
            def _():
                pl.semaphore_wait(barrier, seqs - 1 + half + 2)

            @pl.when(jnp.logical_not(proxy))
            def _():
                pl.semaphore_wait(barrier, seqs - 1 + half)

            @pl.when(core == 0)
            def _():
                log_copy(seq + 1).start()

        if g < GROUPS:

            @pl.when(core == 0)
            def _(g=g):
                pair_copy(seq + 1, g).start()

        if g > 0:

            @pl.when(core == 1)
            def _(g=g - 1):
                if g == 0:
                    log_copy(seq).wait_recv()
                pair_copy(seq, g).wait_recv()
                each_head(g, add_pair)

                @pl.when((chip == 0) & (seqs > 2))
                def _():
                    state_copy(g).start()

    expert = lax.broadcasted_iota(jnp.int32, (owners, block_len), 0)
    named = [(ids_ref[i : i + 1, :] == expert).astype(F32) for i in range(top)]
    member = sum(named)
    after = (down < across).astype(BF16)
    rank = dot(member.astype(BF16), after)
    info[0] = jnp.where(member > 0.5, rank, -1.0)
    info[1] = sum(
        named[i] * (levels_ref[i : i + 1, :].astype(F32) * (1.0 / 256.0)) for i in range(top)
    )
    info_copy = pltpu.make_async_remote_copy(
        info, info_in.at[line], info_send_sem, info_recv_sem.at[line], {"exp": target}, MESH
    )
    info_copy.start()

    def intra_head(h, _):
        c = head_cum(h)
        cols = head_lanes(h)
        scores = dot(q_ref[:, cols], k_ref[:, cols], ((1,), (1,)))
        gap = c - cum_rows[pl.ds(h, 1), :]
        weight = jnp.where(down >= across, jnp.exp(jnp.minimum(gap, 0.0)), 0.0)
        probs = (scores * weight).astype(BF16)
        h_res[:, cols] = dot(probs, v_ref[:, cols])
        return 0

    lax.fori_loop(0, heads, intra_head, 0, unroll=per_group)

    slot = lax.broadcasted_iota(jnp.int32, (cap, block_len), 0).astype(F32)
    same = (down == across).astype(BF16)

    def slots(at, source):
        spread = []
        for n in range(half):
            hit = source[0, pl.ds(base + n, 1), :] == slot
            pick[at, n] = jnp.where(hit, 1.0, 0.0).astype(BF16)
            spread.append(jnp.where(hit, source[1, pl.ds(base + n, 1), :], 0.0).astype(BF16))
        mix[at] = dot(same, jnp.concatenate(spread, axis=0), ((1,), (1,))).astype(BF16)

    slots(0, info)

    @pl.when(proxy)
    def _():
        for i in range(2):
            pltpu.make_async_remote_copy(
                info, info_in.at[i], info_send_sem, info_recv_sem.at[i], {"exp": target}, MESH
            ).wait_recv()
            slots(1 + i, info_in.at[i])

    def add_state(h, _):
        decay = jnp.exp(logs[pl.ds(h, 1), :] + logs_before[pl.ds(h, 1), :])
        state_out[h] = (decay * state_in[h].astype(F32) + contrib[h]).astype(BF16)
        return 0

    def join(h, _):
        carried[h] = (
            decay_row(logs_before, h) * state_in[h].astype(F32) + pair_in[h].astype(F32)
        ).astype(BF16)
        return 0

    def carry(g):
        to, before, passed = group(carried, g), group(pair_in, g), group(state_in, g)

        @pl.when((chip > 0) & (core != g % 2))
        def _():
            state_copy(g).wait_recv()

        @pl.when((core == 1) & (chip > 0) & (chip < seqs // 2 - 1))
        def _():
            each_head(g, add_state)
            state_copy(g).start()

        @pl.when((core == 0) & (chip == 0))
        def _():
            to[...] = jnp.zeros_like(to)

        @pl.when((core == 0) & (chip > 0))
        def _():
            to[...] = passed[...]

        @pl.when((core == 1) & (chip == 0))
        def _():
            to[...] = before[...]

        @pl.when((core == 1) & (chip > 0))
        def _():
            each_head(g, join)

    def inter_head(h, squares):
        c = head_cum(h)
        cols = head_lanes(h)
        raw = h_res[:, cols] + jnp.exp(c) * dot(q_ref[:, cols], carried[h])
        scale = lax.rsqrt(jnp.mean(raw * raw, axis=1, keepdims=True) + 1e-6)
        res = x_ref[:, cols].astype(F32) + raw * scale * attn_gain_ref[:, cols]
        h_res[:, cols] = res
        return squares + res * res

    for g in range(GROUPS):

        @pl.when((chip > 0) & (core == g % 2))
        def _(g=g):
            state_copy(g).wait_recv()
            pass_copy(g).start()

    squares = jnp.zeros((block_len, dh), F32)
    for g in range(GROUPS):
        carry(g)
        squares = each_head(g, inter_head, squares)
    scale = lax.rsqrt(jnp.sum(squares, axis=1, keepdims=True) * (1.0 / width) + 1e-6)

    def part_cols(c):
        return pl.ds(c * tile, tile)

    def relay_copy(c, i):
        return pltpu.make_async_remote_copy(
            normed.at[c],
            relay.at[i, c],
            relay_send_sem.at[c],
            relay_recv_sem.at[i, c],
            {"exp": target},
            MESH,
        )

    def part_copy(c, i):
        return pltpu.make_async_remote_copy(
            part_out.at[i, c],
            part_in.at[c],
            part_send_sem.at[i, c],
            part_recv_sem.at[c],
            {"exp": client(i)},
            MESH,
        )

    def go_copy(peer, slot):
        return pltpu.make_async_remote_copy(
            send.at[peer],
            recv.at[0, slot],
            go_send_sem.at[peer],
            go_recv_sem.at[slot],
            {"exp": base + peer},
            MESH,
        )

    def back_copy(peer, slot):
        return pltpu.make_async_remote_copy(
            done.at[0, peer],
            back.at[slot],
            back_send_sem.at[peer],
            back_recv_sem.at[slot],
            {"exp": base + peer},
            MESH,
        )

    def go_on_copy(c, i, peer, slot):
        return pltpu.make_async_remote_copy(
            send_on.at[i, peer, c],
            recv.at[1, slot, c],
            go_on_send_sem.at[i, peer, c],
            go_on_recv_sem.at[slot, c],
            {"exp": base + peer},
            MESH,
        )

    def back_on_copy(c, i, slot, at, peer):
        return pltpu.make_async_remote_copy(
            done.at[1, slot, c],
            back_on.at[i, at, c],
            back_on_send_sem.at[slot, c],
            back_on_recv_sem.at[i, at, c],
            {"exp": base + peer},
            MESH,
        )

    def each_peer(action):
        def one(j, _):
            action(flip(place, half - 1 - j, bits))
            return 0

        lax.fori_loop(0, half - 1, one, 0)

    def each_slot(action, here=None):
        def one(n, _):
            at, i = proxy_place(lax.div(n, 2)), lax.rem(n, 2)

            @pl.when(at != place)
            def _():
                action(n, at, i)

            if here is not None:

                @pl.when(at == place)
                def _():
                    here(n, i)

            return 0

        lax.fori_loop(0, half, one, 0)

    def picked(at, source):
        rows = dot(pick[at].reshape(half * cap, block_len), source[...])
        return rows.astype(BF16).reshape(half, cap, tile)

    def run_up(at):
        def one(n, _):
            cols = pl.ds(pl.multiple_of(n * 256, 256), 256)
            gate_part = up_part = 0.0
            for c in range(parts):
                rows = recv[at, :, c].reshape(half * cap, tile)
                gate_part = gate_part + dot(rows, wg[part_cols(c), cols])
                up_part = up_part + dot(rows, wu[part_cols(c), cols])
            act[at, :, cols] = (gate_part / (1.0 + jnp.exp(-gate_part)) * up_part).astype(BF16)
            return 0

        lax.fori_loop(0, ff // 256, one, 0)

    def run_down(at, c):
        rows = dot(act[at], wd[:, part_cols(c)]).astype(BF16)
        done[at, :, c] = rows.reshape(half, cap, tile)

    for c in range(parts):
        normed[c] = (h_res[:, part_cols(c)] * scale * norm_gain_ref[:, part_cols(c)]).astype(BF16)
        relay_copy(c, line).start()
    for c in range(parts):
        send[:, c] = picked(0, normed.at[c])
        recv[0, place, c] = send[place, c]
    each_peer(lambda peer: go_copy(peer, place).start())
    for copy in weight_copies:
        copy.wait()

    for c in range(parts):
        if c == parts - 1:
            each_peer(lambda peer: go_copy(peer, peer).wait_recv())
            run_up(0)

        @pl.when(proxy)
        def _(c=c):
            for i in range(2):
                slot_here = low * 2 + i
                relay_copy(c, i).wait_recv()
                send_on[i, :, c] = picked(1 + i, relay.at[i, c])
                recv[1, slot_here, c] = send_on[i, place, c]
                each_peer(lambda peer: go_on_copy(c, i, peer, slot_here).start())

    for c in range(parts):
        each_slot(lambda n, at, i, c=c: go_on_copy(c, i, at, n).wait_recv())
    run_up(1)
    for c in range(parts):
        run_down(1, c)

        def keep(n, i, c=c):
            back_on[i, place, c] = done[1, n, c]

        each_slot(lambda n, at, i, c=c: back_on_copy(c, i, n, place, at).start(), keep)
    for c in range(parts):
        run_down(0, c)
        back[place, c] = done[0, place, c]
    each_peer(lambda peer: back_copy(peer, place).start())

    @pl.when(proxy)
    def _():
        for c in range(parts):
            for i in range(2):
                each_peer(lambda peer: back_on_copy(c, i, peer, peer, peer).wait_recv())
                rows = back_on[i, :, c].reshape(half * cap, tile)
                part_out[i, c] = dot(mix[1 + i], rows).astype(BF16)
                part_copy(c, i).start()

    each_peer(lambda peer: back_copy(peer, peer).wait_recv())
    for c in range(parts):
        h_res[:, part_cols(c)] += dot(mix[0], back[:, c].reshape(half * cap, tile))
    for c in range(parts):
        part_copy(c, 0).wait_recv()
        out_ref[:, part_cols(c)] = (h_res[:, part_cols(c)] + part_in[c].astype(F32)).astype(BF16)

    info_copy.wait_send()
    each_peer(lambda peer: go_copy(peer, place).wait_send())
    each_peer(lambda peer: back_copy(peer, place).wait_send())
    for c in range(parts):
        relay_copy(c, line).wait_send()
        each_slot(lambda n, at, i, c=c: back_on_copy(c, i, n, place, at).wait_send())

    @pl.when(proxy)
    def _():
        for c in range(parts):
            for i in range(2):
                part_copy(c, i).wait_send()
                each_peer(lambda peer: go_on_copy(c, i, peer, 0).wait_send())

    @pl.when(core == 0)
    def _():
        log_copy(seq + 1).wait_send()
        for g in range(GROUPS):
            pair_copy(seq + 1, g).wait_send()

    @pl.when((core == 1) & (chip < seqs // 2 - 1))
    def _():
        for g in range(GROUPS):
            state_copy(g).wait_send()

    for g in range(GROUPS):

        @pl.when((chip > 0) & (core == g % 2))
        def _(g=g):
            pass_copy(g).wait_send()


def per_device(
    layer_input,
    queries,
    keys_in,
    values_in,
    decay_rate,
    attn_gain,
    norm_gain,
    expert_ids,
    gate_levels,
    w_gate,
    w_up,
    w_down,
):
    block_len, width = layer_input.shape[1:]
    heads = decay_rate.shape[2]
    dh = width // heads
    top = expert_ids.shape[2]
    ff = w_gate.shape[2]
    owners = lax.axis_size("exp")
    seqs = lax.axis_size("seq")
    half = owners // 2
    cap = -(-(3 * block_len // owners) // 16) * 16
    tile = width // PARTS
    vmem = pl.BlockSpec(memory_space=pltpu.VMEM)
    hbm = pl.BlockSpec(memory_space=pl.ANY)
    state = pltpu.VMEM((heads, dh, dh), BF16)
    rows = pltpu.VMEM((half, PARTS, cap, tile), BF16)
    two_rows = pltpu.VMEM((2, half, PARTS, cap, tile), BF16)
    columns = pltpu.VMEM((PARTS, block_len, tile), BF16)
    two_columns = pltpu.VMEM((2, PARTS, block_len, tile), BF16)
    known = pltpu.VMEM((2, owners, block_len), F32)
    dma = pltpu.SemaphoreType.DMA
    out = pl.pallas_call(
        functools.partial(layer_kernel, (owners, cap, seqs, heads, top)),
        out_shape=jax.ShapeDtypeStruct((block_len, width), BF16),
        in_specs=[vmem] * 9 + [hbm] * 3,
        out_specs=vmem,
        scratch_shapes=[
            pltpu.VMEM((width, ff), BF16),
            pltpu.VMEM((width, ff), BF16),
            pltpu.VMEM((ff, width), BF16),
            pltpu.VMEM((block_len, heads), F32),
            pltpu.VMEM((heads, block_len), F32),
            pltpu.VMEM((heads, dh), F32),
            pltpu.VMEM((heads, dh), F32),
            pltpu.VMEM((heads, dh, dh), F32),
            state,
            state,
            state,
            state,
            pltpu.VMEM((block_len, width), F32),
            columns,
            two_columns,
            known,
            pltpu.VMEM((2, 2, owners, block_len), F32),
            pltpu.VMEM((3, half, cap, block_len), BF16),
            pltpu.VMEM((3, block_len, half * cap), BF16),
            rows,
            two_rows,
            two_rows,
            pltpu.VMEM((2, half * cap, ff), BF16),
            two_rows,
            rows,
            two_rows,
            two_columns,
            columns,
            dma((3,)),
            dma((2, GROUPS)),
            dma((2,)),
            dma((GROUPS,)),
            dma((GROUPS,)),
            dma((GROUPS,)),
            dma,
            dma((2,)),
            dma((PARTS,)),
            dma((2, PARTS)),
            dma((half,)),
            dma((half,)),
            dma((2, half, PARTS)),
            dma((half, PARTS)),
            dma((half,)),
            dma((half,)),
            dma((half, PARTS)),
            dma((2, half, PARTS)),
            dma((2, PARTS)),
            dma((PARTS,)),
        ],
        compiler_params=pltpu.CompilerParams(
            collective_id=0, has_side_effects=True, vmem_limit_bytes=56 * 1024 * 1024
        ),
    )(
        layer_input[0],
        queries[0],
        keys_in[0],
        values_in[0],
        decay_rate[0].T,
        attn_gain[None],
        norm_gain[None],
        expert_ids[0].T,
        gate_levels[0].T,
        w_gate[0],
        w_up[0],
        w_down[0],
    )
    return out[None]


def solution(mesh):
    tokens = P("exp", "seq", None)
    experts = P("exp", None, None)
    return jax.shard_map(
        per_device,
        mesh=mesh,
        in_specs=(tokens,) * 5 + (P(), P()) + (tokens,) * 2 + (experts,) * 3,
        out_specs=tokens,
        check_vma=False,
    )
```

```python
import functools

import jax
import jax.numpy as jnp
from jax import lax
from jax.experimental import pallas as pl
from jax.experimental.pallas import tpu as pltpu
from jax.sharding import PartitionSpec as P

MESH = pl.DeviceIdType.MESH
F32 = jnp.float32
BF16 = jnp.bfloat16
PARTS = 8
LAG = 2
GROUPS = 4


def flip(index, mask, bits):
    result = 0
    for b in range(bits):
        p = 1 << b
        result = result + p * lax.rem(lax.div(index, p) + lax.div(mask, p), 2)
    return result


def dot(a, b, contract=((1,), (0,)), **kw):
    return lax.dot_general(a, b, (contract, ((), ())), preferred_element_type=F32, **kw)


def layer_kernel(
    dims,
    x_ref,
    q_ref,
    k_ref,
    v_ref,
    decay_ref,
    attn_gain_ref,
    norm_gain_ref,
    ids_ref,
    levels_ref,
    wg_hbm,
    wu_hbm,
    wd_hbm,
    out_ref,
    wg,
    wu,
    wd,
    cum,
    cum_rows,
    logs,
    logs_before,
    contrib,
    state_out,
    pair_in,
    state_in,
    carried,
    h_res,
    normed,
    relay,
    info,
    info_in,
    pick,
    mix,
    send,
    send_on,
    recv,
    act,
    gate_sum,
    up_sum,
    done,
    back,
    back_on,
    part_out,
    part_in,
    weight_sem,
    pair_sem,
    log_sem,
    state_send_sem,
    state_recv_sem,
    state_pass_sem,
    info_send_sem,
    info_recv_sem,
    relay_send_sem,
    relay_recv_sem,
    go_send_sem,
    go_recv_sem,
    go_on_send_sem,
    go_on_recv_sem,
    back_send_sem,
    back_recv_sem,
    back_on_send_sem,
    back_on_recv_sem,
    part_send_sem,
    part_recv_sem,
):
    owners, cap, seqs, heads, top = dims
    block_len, width = x_ref.shape
    dh = width // heads
    ff = wg.shape[1]
    half = owners // 2
    bits = half.bit_length() - 1
    parts, _, tile = normed.shape
    seq = lax.axis_index("seq")
    mine = lax.axis_index("exp")
    chip = lax.div(seq, 2)
    core = lax.rem(seq, 2)
    place = lax.rem(mine, half)
    base = mine - place
    quarter = half // 2
    side = lax.div(mine, half)
    line = lax.div(place, quarter)
    low = lax.rem(place, quarter)
    proxy = side + line == 1
    target = (1 - side) * half + side * quarter + low

    def client(i):
        return (1 - side) * half + i * quarter + low

    def proxy_place(i):
        return (1 - side) * quarter + i

    weight_copies = [
        pltpu.make_async_copy(hbm, vmem, weight_sem.at[i])
        for i, (hbm, vmem) in enumerate(((wg_hbm, wg), (wu_hbm, wu), (wd_hbm, wd)))
    ]
    for copy in weight_copies:
        copy.start()

    barrier = pltpu.get_barrier_semaphore()
    for step in range(1, seqs):
        pl.semaphore_signal(
            barrier, inc=1, device_id={"seq": lax.rem(seq + step, seqs)}, device_id_type=MESH
        )
    for step in range(1, half):
        pl.semaphore_signal(
            barrier,
            inc=1,
            device_id={"exp": base + lax.rem(place + step, half)},
            device_id_type=MESH,
        )
    pl.semaphore_signal(barrier, inc=1, device_id={"exp": target}, device_id_type=MESH)

    @pl.when(proxy)
    def _():
        for i in range(2):
            pl.semaphore_signal(barrier, inc=1, device_id={"exp": client(i)}, device_id_type=MESH)


    down = lax.broadcasted_iota(jnp.int32, (block_len, block_len), 0)
    across = lax.broadcasted_iota(jnp.int32, (block_len, block_len), 1)
    lower = (down >= across).astype(F32)
    upper = (down <= across).astype(F32)
    rate = -decay_ref[...]
    cum[...] = dot(lower, rate, ((1,), (1,)), precision=lax.Precision.HIGHEST)
    cum_rows[...] = dot(rate, upper, precision=lax.Precision.HIGHEST)
    logs[...] = jnp.broadcast_to(cum_rows[:, block_len - 1 : block_len], logs.shape)
    lanes = lax.broadcasted_iota(jnp.int32, (block_len, heads), 1)

    def head_cum(h):
        return jnp.sum(jnp.where(lanes == h, cum[...], 0.0), axis=1, keepdims=True)

    def head_lanes(h):
        return pl.ds(pl.multiple_of(h * dh, dh), dh)

    def contrib_head(h, _):
        c = head_cum(h)
        cols = head_lanes(h)
        weight = jnp.exp(c[block_len - 1 :, :] - c)
        weighted = (k_ref[:, cols].astype(F32) * weight).astype(BF16)
        value = dot(weighted, v_ref[:, cols], ((0,), (0,)))
        contrib[h] = value
        state_out[h] = value.astype(BF16)
        return 0

    per_group = heads // GROUPS

    def group(ref, g):
        return ref.at[pl.ds(g * per_group, per_group)]

    def each_head(g, body, start=0):
        return lax.fori_loop(g * per_group, (g + 1) * per_group, body, start, unroll=per_group)

    def pair_copy(target, g):
        return pltpu.make_async_remote_copy(
            group(state_out, g),
            group(pair_in, g),
            pair_sem.at[0, g],
            pair_sem.at[1, g],
            {"seq": target},
            MESH,
        )

    def log_copy(target):
        return pltpu.make_async_remote_copy(
            logs, logs_before, log_sem.at[0], log_sem.at[1], {"seq": target}, MESH
        )

    def state_copy(g):
        return pltpu.make_async_remote_copy(
            group(state_out, g),
            group(state_in, g),
            state_send_sem.at[g],
            state_recv_sem.at[g],
            {"seq": lax.rem(seq + 1 + g % 2, seqs)},
            MESH,
        )

    def pass_copy(g):
        return pltpu.make_async_remote_copy(
            group(state_in, g),
            group(state_in, g),
            state_pass_sem.at[g],
            state_recv_sem.at[g],
            {"seq": seq + 1 - 2 * core},
            MESH,
        )

    def decay_row(ref, h):
        return jnp.exp(ref[pl.ds(h, 1), :])

    def add_pair(h, _):
        both = decay_row(logs, h) * pair_in[h].astype(F32) + contrib[h]
        contrib[h] = both
        state_out[h] = both.astype(BF16)
        return 0

    for g in range(GROUPS + 1):
        if g < GROUPS:
            each_head(g, contrib_head)
        if g == 0:

            @pl.when(proxy)
            def _():
                pl.semaphore_wait(barrier, seqs - 1 + half + 2)

            @pl.when(jnp.logical_not(proxy))
            def _():
                pl.semaphore_wait(barrier, seqs - 1 + half)

            @pl.when(core == 0)
            def _():
                log_copy(seq + 1).start()

        if g < GROUPS:

            @pl.when(core == 0)
            def _(g=g):
                pair_copy(seq + 1, g).start()

        if g > 0:

            @pl.when(core == 1)
            def _(g=g - 1):
                if g == 0:
                    log_copy(seq).wait_recv()
                pair_copy(seq, g).wait_recv()
                each_head(g, add_pair)

                @pl.when((chip == 0) & (seqs > 2))
                def _():
                    state_copy(g).start()

    expert = lax.broadcasted_iota(jnp.int32, (owners, block_len), 0)
    named = [(ids_ref[i : i + 1, :] == expert).astype(F32) for i in range(top)]
    member = sum(named)
    after = (down < across).astype(BF16)
    rank = dot(member.astype(BF16), after)
    info[0] = jnp.where(member > 0.5, rank, -1.0)
    info[1] = sum(
        named[i] * (levels_ref[i : i + 1, :].astype(F32) * (1.0 / 256.0)) for i in range(top)
    )
    info_copy = pltpu.make_async_remote_copy(
        info, info_in.at[line], info_send_sem, info_recv_sem.at[line], {"exp": target}, MESH
    )
    info_copy.start()

    def intra_head(h, _):
        c = head_cum(h)
        cols = head_lanes(h)
        scores = dot(q_ref[:, cols], k_ref[:, cols], ((1,), (1,)))
        gap = c - cum_rows[pl.ds(h, 1), :]
        weight = jnp.where(down >= across, jnp.exp(jnp.minimum(gap, 0.0)), 0.0)
        probs = (scores * weight).astype(BF16)
        h_res[:, cols] = dot(probs, v_ref[:, cols])
        return 0

    lax.fori_loop(0, heads, intra_head, 0, unroll=per_group)

    slot = lax.broadcasted_iota(jnp.int32, (cap, block_len), 0).astype(F32)
    same = (down == across).astype(BF16)

    def slots(at, source):
        spread = []
        for n in range(half):
            hit = source[0, pl.ds(base + n, 1), :] == slot
            pick[at, n] = jnp.where(hit, 1.0, 0.0).astype(BF16)
            spread.append(jnp.where(hit, source[1, pl.ds(base + n, 1), :], 0.0).astype(BF16))
        mix[at] = dot(same, jnp.concatenate(spread, axis=0), ((1,), (1,))).astype(BF16)

    slots(0, info)

    @pl.when(proxy)
    def _():
        for i in range(2):
            pltpu.make_async_remote_copy(
                info, info_in.at[i], info_send_sem, info_recv_sem.at[i], {"exp": target}, MESH
            ).wait_recv()
            slots(1 + i, info_in.at[i])

    def add_state(h, _):
        decay = jnp.exp(logs[pl.ds(h, 1), :] + logs_before[pl.ds(h, 1), :])
        state_out[h] = (decay * state_in[h].astype(F32) + contrib[h]).astype(BF16)
        return 0

    def join(h, _):
        carried[h] = (
            decay_row(logs_before, h) * state_in[h].astype(F32) + pair_in[h].astype(F32)
        ).astype(BF16)
        return 0

    def carry(g):
        to, before, passed = group(carried, g), group(pair_in, g), group(state_in, g)

        @pl.when((chip > 0) & (core != g % 2))
        def _():
            state_copy(g).wait_recv()

        @pl.when((core == 1) & (chip > 0) & (chip < seqs // 2 - 1))
        def _():
            each_head(g, add_state)
            state_copy(g).start()

        @pl.when((core == 0) & (chip == 0))
        def _():
            to[...] = jnp.zeros_like(to)

        @pl.when((core == 0) & (chip > 0))
        def _():
            to[...] = passed[...]

        @pl.when((core == 1) & (chip == 0))
        def _():
            to[...] = before[...]

        @pl.when((core == 1) & (chip > 0))
        def _():
            each_head(g, join)

    def inter_head(h, squares):
        c = head_cum(h)
        cols = head_lanes(h)
        raw = h_res[:, cols] + jnp.exp(c) * dot(q_ref[:, cols], carried[h])
        scale = lax.rsqrt(jnp.mean(raw * raw, axis=1, keepdims=True) + 1e-6)
        res = x_ref[:, cols].astype(F32) + raw * scale * attn_gain_ref[:, cols]
        h_res[:, cols] = res
        return squares + res * res

    for g in range(GROUPS):

        @pl.when((chip > 0) & (core == g % 2))
        def _(g=g):
            state_copy(g).wait_recv()
            pass_copy(g).start()

    squares = jnp.zeros((block_len, dh), F32)
    for g in range(GROUPS):
        carry(g)
        squares = each_head(g, inter_head, squares)
    scale = lax.rsqrt(jnp.sum(squares, axis=1, keepdims=True) * (1.0 / width) + 1e-6)

    def part_cols(c):
        return pl.ds(c * tile, tile)

    def relay_copy(c, i):
        return pltpu.make_async_remote_copy(
            normed.at[c],
            relay.at[i, c],
            relay_send_sem.at[c],
            relay_recv_sem.at[i, c],
            {"exp": target},
            MESH,
        )

    def part_copy(c, i):
        return pltpu.make_async_remote_copy(
            part_out.at[i, c],
            part_in.at[c],
            part_send_sem.at[i, c],
            part_recv_sem.at[c],
            {"exp": client(i)},
            MESH,
        )

    def go_copy(peer, slot):
        return pltpu.make_async_remote_copy(
            send.at[peer],
            recv.at[0, slot],
            go_send_sem.at[peer],
            go_recv_sem.at[slot],
            {"exp": base + peer},
            MESH,
        )

    def back_copy(peer, slot):
        return pltpu.make_async_remote_copy(
            done.at[0, peer],
            back.at[slot],
            back_send_sem.at[peer],
            back_recv_sem.at[slot],
            {"exp": base + peer},
            MESH,
        )

    def go_on_copy(c, i, peer, slot):
        return pltpu.make_async_remote_copy(
            send_on.at[i, peer, c],
            recv.at[1, slot, c],
            go_on_send_sem.at[i, peer, c],
            go_on_recv_sem.at[slot, c],
            {"exp": base + peer},
            MESH,
        )

    def back_on_copy(c, i, slot, at, peer):
        return pltpu.make_async_remote_copy(
            done.at[1, slot, c],
            back_on.at[i, at, c],
            back_on_send_sem.at[slot, c],
            back_on_recv_sem.at[i, at, c],
            {"exp": base + peer},
            MESH,
        )

    def each_peer(action):
        def one(j, _):
            action(flip(place, half - 1 - j, bits))
            return 0

        lax.fori_loop(0, half - 1, one, 0)

    def each_slot(action, here=None):
        def one(n, _):
            at, i = proxy_place(lax.div(n, 2)), lax.rem(n, 2)

            @pl.when(at != place)
            def _():
                action(n, at, i)

            if here is not None:

                @pl.when(at == place)
                def _():
                    here(n, i)

            return 0

        lax.fori_loop(0, half, one, 0)

    def picked(at, source):
        rows = dot(pick[at].reshape(half * cap, block_len), source[...])
        return rows.astype(BF16).reshape(half, cap, tile)

    def activate(gate_part, up_part):
        return (gate_part / (1.0 + jnp.exp(-gate_part)) * up_part).astype(BF16)

    def each_hidden(action):
        def one(n, _):
            action(pl.ds(pl.multiple_of(n * 256, 256), 256))
            return 0

        lax.fori_loop(0, ff // 256, one, 0)

    def run_up():
        def one(cols):
            gate_part = up_part = 0.0
            for c in range(parts):
                rows = recv[0, :, c].reshape(half * cap, tile)
                gate_part = gate_part + dot(rows, wg[part_cols(c), cols])
                up_part = up_part + dot(rows, wu[part_cols(c), cols])
            act[0, :, cols] = activate(gate_part, up_part)

        each_hidden(one)

    def add_up(c):
        each_slot(lambda n, at, i: go_on_copy(c, i, at, n).wait_recv())

        def one(cols):
            rows = recv[1, :, c].reshape(half * cap, tile)
            gate_part = dot(rows, wg[part_cols(c), cols])
            up_part = dot(rows, wu[part_cols(c), cols])
            if c > 0:
                gate_part = gate_part + gate_sum[:, cols]
                up_part = up_part + up_sum[:, cols]
            if c < parts - 1:
                gate_sum[:, cols] = gate_part
                up_sum[:, cols] = up_part
            else:
                act[1, :, cols] = activate(gate_part, up_part)

        each_hidden(one)

    def run_down(at, c):
        rows = dot(act[at], wd[:, part_cols(c)]).astype(BF16)
        done[at, :, c] = rows.reshape(half, cap, tile)

    for c in range(parts):
        normed[c] = (h_res[:, part_cols(c)] * scale * norm_gain_ref[:, part_cols(c)]).astype(BF16)
        relay_copy(c, line).start()
    for c in range(parts):
        send[:, c] = picked(0, normed.at[c])
        recv[0, place, c] = send[place, c]
    each_peer(lambda peer: go_copy(peer, place).start())
    for copy in weight_copies:
        copy.wait()

    for c in range(parts):
        @pl.when(proxy)
        def _(c=c):
            for i in range(2):
                slot_here = low * 2 + i
                relay_copy(c, i).wait_recv()
                send_on[i, :, c] = picked(1 + i, relay.at[i, c])
                recv[1, slot_here, c] = send_on[i, place, c]
                each_peer(lambda peer: go_on_copy(c, i, peer, slot_here).start())

        if c >= LAG:
            add_up(c - LAG)

    each_peer(lambda peer: go_copy(peer, peer).wait_recv())
    run_up()
    for c in range(parts - LAG, parts):
        add_up(c)
    for c in range(parts):
        run_down(1, c)

        def keep(n, i, c=c):
            back_on[i, place, c] = done[1, n, c]

        each_slot(lambda n, at, i, c=c: back_on_copy(c, i, n, place, at).start(), keep)
    for c in range(parts):
        run_down(0, c)
        back[place, c] = done[0, place, c]
    each_peer(lambda peer: back_copy(peer, place).start())

    @pl.when(proxy)
    def _():
        for c in range(parts):
            for i in range(2):
                each_peer(lambda peer: back_on_copy(c, i, peer, peer, peer).wait_recv())
                rows = back_on[i, :, c].reshape(half * cap, tile)
                part_out[i, c] = dot(mix[1 + i], rows).astype(BF16)
                part_copy(c, i).start()

    each_peer(lambda peer: back_copy(peer, peer).wait_recv())
    for c in range(parts):
        h_res[:, part_cols(c)] += dot(mix[0], back[:, c].reshape(half * cap, tile))
    for c in range(parts):
        part_copy(c, 0).wait_recv()
        out_ref[:, part_cols(c)] = (h_res[:, part_cols(c)] + part_in[c].astype(F32)).astype(BF16)

    info_copy.wait_send()
    each_peer(lambda peer: go_copy(peer, place).wait_send())
    each_peer(lambda peer: back_copy(peer, place).wait_send())
    for c in range(parts):
        relay_copy(c, line).wait_send()
        each_slot(lambda n, at, i, c=c: back_on_copy(c, i, n, place, at).wait_send())

    @pl.when(proxy)
    def _():
        for c in range(parts):
            for i in range(2):
                part_copy(c, i).wait_send()
                each_peer(lambda peer: go_on_copy(c, i, peer, 0).wait_send())

    @pl.when(core == 0)
    def _():
        log_copy(seq + 1).wait_send()
        for g in range(GROUPS):
            pair_copy(seq + 1, g).wait_send()

    @pl.when((core == 1) & (chip < seqs // 2 - 1))
    def _():
        for g in range(GROUPS):
            state_copy(g).wait_send()

    for g in range(GROUPS):

        @pl.when((chip > 0) & (core == g % 2))
        def _(g=g):
            pass_copy(g).wait_send()


def per_device(
    layer_input,
    queries,
    keys_in,
    values_in,
    decay_rate,
    attn_gain,
    norm_gain,
    expert_ids,
    gate_levels,
    w_gate,
    w_up,
    w_down,
):
    block_len, width = layer_input.shape[1:]
    heads = decay_rate.shape[2]
    dh = width // heads
    top = expert_ids.shape[2]
    ff = w_gate.shape[2]
    owners = lax.axis_size("exp")
    seqs = lax.axis_size("seq")
    half = owners // 2
    cap = -(-(3 * block_len // owners) // 16) * 16
    tile = width // PARTS
    vmem = pl.BlockSpec(memory_space=pltpu.VMEM)
    hbm = pl.BlockSpec(memory_space=pl.ANY)
    state = pltpu.VMEM((heads, dh, dh), BF16)
    rows = pltpu.VMEM((half, PARTS, cap, tile), BF16)
    two_rows = pltpu.VMEM((2, half, PARTS, cap, tile), BF16)
    columns = pltpu.VMEM((PARTS, block_len, tile), BF16)
    two_columns = pltpu.VMEM((2, PARTS, block_len, tile), BF16)
    known = pltpu.VMEM((2, owners, block_len), F32)
    dma = pltpu.SemaphoreType.DMA
    out = pl.pallas_call(
        functools.partial(layer_kernel, (owners, cap, seqs, heads, top)),
        out_shape=jax.ShapeDtypeStruct((block_len, width), BF16),
        in_specs=[vmem] * 9 + [hbm] * 3,
        out_specs=vmem,
        scratch_shapes=[
            pltpu.VMEM((width, ff), BF16),
            pltpu.VMEM((width, ff), BF16),
            pltpu.VMEM((ff, width), BF16),
            pltpu.VMEM((block_len, heads), F32),
            pltpu.VMEM((heads, block_len), F32),
            pltpu.VMEM((heads, dh), F32),
            pltpu.VMEM((heads, dh), F32),
            pltpu.VMEM((heads, dh, dh), F32),
            state,
            state,
            state,
            state,
            pltpu.VMEM((block_len, width), F32),
            columns,
            two_columns,
            known,
            pltpu.VMEM((2, 2, owners, block_len), F32),
            pltpu.VMEM((3, half, cap, block_len), BF16),
            pltpu.VMEM((3, block_len, half * cap), BF16),
            rows,
            two_rows,
            two_rows,
            pltpu.VMEM((2, half * cap, ff), BF16),
            pltpu.VMEM((half * cap, ff), F32),
            pltpu.VMEM((half * cap, ff), F32),
            two_rows,
            rows,
            two_rows,
            two_columns,
            columns,
            dma((3,)),
            dma((2, GROUPS)),
            dma((2,)),
            dma((GROUPS,)),
            dma((GROUPS,)),
            dma((GROUPS,)),
            dma,
            dma((2,)),
            dma((PARTS,)),
            dma((2, PARTS)),
            dma((half,)),
            dma((half,)),
            dma((2, half, PARTS)),
            dma((half, PARTS)),
            dma((half,)),
            dma((half,)),
            dma((half, PARTS)),
            dma((2, half, PARTS)),
            dma((2, PARTS)),
            dma((PARTS,)),
        ],
        compiler_params=pltpu.CompilerParams(
            collective_id=0, has_side_effects=True, vmem_limit_bytes=56 * 1024 * 1024
        ),
    )(
        layer_input[0],
        queries[0],
        keys_in[0],
        values_in[0],
        decay_rate[0].T,
        attn_gain[None],
        norm_gain[None],
        expert_ids[0].T,
        gate_levels[0].T,
        w_gate[0],
        w_up[0],
        w_down[0],
    )
    return out[None]


def solution(mesh):
    tokens = P("exp", "seq", None)
    experts = P("exp", None, None)
    return jax.shard_map(
        per_device,
        mesh=mesh,
        in_specs=(tokens,) * 5 + (P(), P()) + (tokens,) * 2 + (experts,) * 3,
        out_specs=tokens,
        check_vma=False,
    )
```

```python
import functools

import jax
import jax.numpy as jnp
from jax import lax
from jax.experimental import pallas as pl
from jax.experimental.pallas import tpu as pltpu
from jax.sharding import PartitionSpec as P

MESH = pl.DeviceIdType.MESH
F32 = jnp.float32
BF16 = jnp.bfloat16
PARTS = 8
LAG = 2
GROUPS = 4


def flip(index, mask, bits):
    result = 0
    for b in range(bits):
        p = 1 << b
        result = result + p * lax.rem(lax.div(index, p) + lax.div(mask, p), 2)
    return result


def dot(a, b, contract=((1,), (0,)), **kw):
    return lax.dot_general(a, b, (contract, ((), ())), preferred_element_type=F32, **kw)


def layer_kernel(
    dims,
    x_ref,
    q_ref,
    k_ref,
    v_ref,
    decay_ref,
    attn_gain_ref,
    norm_gain_ref,
    ids_ref,
    levels_ref,
    wg_hbm,
    wu_hbm,
    wd_hbm,
    out_ref,
    wg,
    wu,
    wd,
    cum,
    cum_rows,
    logs,
    logs_before,
    contrib,
    state_out,
    pair_in,
    state_in,
    carried,
    h_res,
    normed,
    relay,
    info,
    info_in,
    pick,
    mix,
    send,
    send_on,
    recv,
    act,
    gate_sum,
    up_sum,
    done,
    back,
    back_on,
    part_out,
    part_in,
    weight_sem,
    pair_sem,
    log_sem,
    state_send_sem,
    state_recv_sem,
    state_pass_sem,
    info_send_sem,
    info_recv_sem,
    relay_send_sem,
    relay_recv_sem,
    go_send_sem,
    go_recv_sem,
    go_on_send_sem,
    go_on_recv_sem,
    back_send_sem,
    back_recv_sem,
    back_on_send_sem,
    back_on_recv_sem,
    part_send_sem,
    part_recv_sem,
):
    owners, cap, seqs, heads, top = dims
    block_len, width = x_ref.shape
    dh = width // heads
    ff = wg.shape[1]
    half = owners // 2
    bits = half.bit_length() - 1
    parts, _, tile = normed.shape
    seq = lax.axis_index("seq")
    mine = lax.axis_index("exp")
    chip = lax.div(seq, 2)
    core = lax.rem(seq, 2)
    place = lax.rem(mine, half)
    base = mine - place
    quarter = half // 2
    side = lax.div(mine, half)
    line = lax.div(place, quarter)
    low = lax.rem(place, quarter)
    proxy = side + line == 1
    target = (1 - side) * half + side * quarter + low

    def client(i):
        return (1 - side) * half + i * quarter + low

    def proxy_place(i):
        return (1 - side) * quarter + i

    weight_copies = [
        pltpu.make_async_copy(hbm, vmem, weight_sem.at[i])
        for i, (hbm, vmem) in enumerate(((wg_hbm, wg), (wu_hbm, wu), (wd_hbm, wd)))
    ]
    for copy in weight_copies:
        copy.start()

    barrier = pltpu.get_barrier_semaphore()
    for step in range(1, seqs):
        pl.semaphore_signal(
            barrier, inc=1, device_id={"seq": lax.rem(seq + step, seqs)}, device_id_type=MESH
        )
    for step in range(1, half):
        pl.semaphore_signal(
            barrier,
            inc=1,
            device_id={"exp": base + lax.rem(place + step, half)},
            device_id_type=MESH,
        )
    pl.semaphore_signal(barrier, inc=1, device_id={"exp": target}, device_id_type=MESH)

    @pl.when(proxy)
    def _():
        for i in range(2):
            pl.semaphore_signal(barrier, inc=1, device_id={"exp": client(i)}, device_id_type=MESH)


    down = lax.broadcasted_iota(jnp.int32, (block_len, block_len), 0)
    across = lax.broadcasted_iota(jnp.int32, (block_len, block_len), 1)
    lower = (down >= across).astype(F32)
    upper = (down <= across).astype(F32)
    rate = -decay_ref[...]
    cum[...] = dot(lower, rate, ((1,), (1,)), precision=lax.Precision.HIGHEST)
    cum_rows[...] = dot(rate, upper, precision=lax.Precision.HIGHEST)
    logs[...] = jnp.broadcast_to(cum_rows[:, block_len - 1 : block_len], logs.shape)
    lanes = lax.broadcasted_iota(jnp.int32, (block_len, heads), 1)

    def head_cum(h):
        return jnp.sum(jnp.where(lanes == h, cum[...], 0.0), axis=1, keepdims=True)

    def head_lanes(h):
        return pl.ds(pl.multiple_of(h * dh, dh), dh)

    def contrib_head(h, _):
        c = head_cum(h)
        cols = head_lanes(h)
        weight = jnp.exp(c[block_len - 1 :, :] - c)
        weighted = (k_ref[:, cols].astype(F32) * weight).astype(BF16)
        value = dot(weighted, v_ref[:, cols], ((0,), (0,)))
        contrib[h] = value
        state_out[h] = value.astype(BF16)
        return 0

    per_group = heads // GROUPS

    def group(ref, g):
        return ref.at[pl.ds(g * per_group, per_group)]

    def each_head(g, body, start=0):
        return lax.fori_loop(g * per_group, (g + 1) * per_group, body, start, unroll=per_group)

    def pair_copy(target, g):
        return pltpu.make_async_remote_copy(
            group(state_out, g),
            group(pair_in, g),
            pair_sem.at[0, g],
            pair_sem.at[1, g],
            {"seq": target},
            MESH,
        )

    def log_copy(target):
        return pltpu.make_async_remote_copy(
            logs, logs_before, log_sem.at[0], log_sem.at[1], {"seq": target}, MESH
        )

    def state_copy(g):
        return pltpu.make_async_remote_copy(
            group(state_out, g),
            group(state_in, g),
            state_send_sem.at[g],
            state_recv_sem.at[g],
            {"seq": lax.rem(seq + 1 + g % 2, seqs)},
            MESH,
        )

    def pass_copy(g):
        return pltpu.make_async_remote_copy(
            group(state_in, g),
            group(state_in, g),
            state_pass_sem.at[g],
            state_recv_sem.at[g],
            {"seq": seq + 1 - 2 * core},
            MESH,
        )

    def decay_row(ref, h):
        return jnp.exp(ref[pl.ds(h, 1), :])

    def add_pair(h, _):
        both = decay_row(logs, h) * pair_in[h].astype(F32) + contrib[h]
        contrib[h] = both
        state_out[h] = both.astype(BF16)
        return 0

    for g in range(GROUPS + 1):
        if g < GROUPS:
            each_head(g, contrib_head)
        if g == 0:

            @pl.when(proxy)
            def _():
                pl.semaphore_wait(barrier, seqs - 1 + half + 2)

            @pl.when(jnp.logical_not(proxy))
            def _():
                pl.semaphore_wait(barrier, seqs - 1 + half)

            @pl.when(core == 0)
            def _():
                log_copy(seq + 1).start()

        if g < GROUPS:

            @pl.when(core == 0)
            def _(g=g):
                pair_copy(seq + 1, g).start()

        if g > 0:

            @pl.when(core == 1)
            def _(g=g - 1):
                if g == 0:
                    log_copy(seq).wait_recv()
                pair_copy(seq, g).wait_recv()
                each_head(g, add_pair)

                @pl.when((chip == 0) & (seqs > 2))
                def _():
                    state_copy(g).start()

    expert = lax.broadcasted_iota(jnp.int32, (owners, block_len), 0)
    named = [(ids_ref[i : i + 1, :] == expert).astype(F32) for i in range(top)]
    member = sum(named)
    after = (down < across).astype(BF16)
    rank = dot(member.astype(BF16), after)
    info[0] = jnp.where(member > 0.5, rank, -1.0)
    info[1] = sum(
        named[i] * (levels_ref[i : i + 1, :].astype(F32) * (1.0 / 256.0)) for i in range(top)
    )
    info_copy = pltpu.make_async_remote_copy(
        info, info_in.at[line], info_send_sem, info_recv_sem.at[line], {"exp": target}, MESH
    )
    info_copy.start()

    def intra_head(h, _):
        c = head_cum(h)
        cols = head_lanes(h)
        scores = dot(q_ref[:, cols], k_ref[:, cols], ((1,), (1,)))
        gap = c - cum_rows[pl.ds(h, 1), :]
        weight = jnp.where(down >= across, jnp.exp(jnp.minimum(gap, 0.0)), 0.0)
        probs = (scores * weight).astype(BF16)
        h_res[:, cols] = dot(probs, v_ref[:, cols])
        return 0

    lax.fori_loop(0, heads, intra_head, 0, unroll=per_group)

    slot = lax.broadcasted_iota(jnp.int32, (cap, block_len), 0).astype(F32)
    same = (down == across).astype(BF16)

    def slots(at, source):
        spread = []
        for n in range(half):
            hit = source[0, pl.ds(base + n, 1), :] == slot
            pick[at, n] = jnp.where(hit, 1.0, 0.0).astype(BF16)
            spread.append(jnp.where(hit, source[1, pl.ds(base + n, 1), :], 0.0).astype(BF16))
        mix[at] = dot(same, jnp.concatenate(spread, axis=0), ((1,), (1,))).astype(BF16)

    def add_state(h, _):
        decay = jnp.exp(logs[pl.ds(h, 1), :] + logs_before[pl.ds(h, 1), :])
        state_out[h] = (decay * state_in[h].astype(F32) + contrib[h]).astype(BF16)
        return 0

    def join(h, _):
        carried[h] = (
            decay_row(logs_before, h) * state_in[h].astype(F32) + pair_in[h].astype(F32)
        ).astype(BF16)
        return 0

    def carry(g):
        to, before, passed = group(carried, g), group(pair_in, g), group(state_in, g)

        @pl.when((chip > 0) & (core != g % 2))
        def _():
            state_copy(g).wait_recv()

        @pl.when((core == 1) & (chip > 0) & (chip < seqs // 2 - 1))
        def _():
            each_head(g, add_state)
            state_copy(g).start()

        @pl.when((core == 0) & (chip == 0))
        def _():
            to[...] = jnp.zeros_like(to)

        @pl.when((core == 0) & (chip > 0))
        def _():
            to[...] = passed[...]

        @pl.when((core == 1) & (chip == 0))
        def _():
            to[...] = before[...]

        @pl.when((core == 1) & (chip > 0))
        def _():
            each_head(g, join)

    def inter_head(h, squares):
        c = head_cum(h)
        cols = head_lanes(h)
        raw = h_res[:, cols] + jnp.exp(c) * dot(q_ref[:, cols], carried[h])
        scale = lax.rsqrt(jnp.mean(raw * raw, axis=1, keepdims=True) + 1e-6)
        res = x_ref[:, cols].astype(F32) + raw * scale * attn_gain_ref[:, cols]
        h_res[:, cols] = res
        return squares + res * res

    for g in range(GROUPS):

        @pl.when((chip > 0) & (core == g % 2))
        def _(g=g):
            state_copy(g).wait_recv()
            pass_copy(g).start()

    squares = jnp.zeros((block_len, dh), F32)
    for g in range(GROUPS):
        carry(g)
        squares = each_head(g, inter_head, squares)
    scale = lax.rsqrt(jnp.sum(squares, axis=1, keepdims=True) * (1.0 / width) + 1e-6)

    def part_cols(c):
        return pl.ds(c * tile, tile)

    def relay_copy(c, i):
        return pltpu.make_async_remote_copy(
            normed.at[c],
            relay.at[i, c],
            relay_send_sem.at[c],
            relay_recv_sem.at[i, c],
            {"exp": target},
            MESH,
        )

    def part_copy(c, i):
        return pltpu.make_async_remote_copy(
            part_out.at[i, c],
            part_in.at[c],
            part_send_sem.at[i, c],
            part_recv_sem.at[c],
            {"exp": client(i)},
            MESH,
        )

    def go_copy(peer, slot):
        return pltpu.make_async_remote_copy(
            send.at[peer],
            recv.at[0, slot],
            go_send_sem.at[peer],
            go_recv_sem.at[slot],
            {"exp": base + peer},
            MESH,
        )

    def back_copy(peer, slot):
        return pltpu.make_async_remote_copy(
            done.at[0, peer],
            back.at[slot],
            back_send_sem.at[peer],
            back_recv_sem.at[slot],
            {"exp": base + peer},
            MESH,
        )

    def go_on_copy(c, i, peer, slot):
        return pltpu.make_async_remote_copy(
            send_on.at[i, peer, c],
            recv.at[1, slot, c],
            go_on_send_sem.at[i, peer, c],
            go_on_recv_sem.at[slot, c],
            {"exp": base + peer},
            MESH,
        )

    def back_on_copy(c, i, slot, at, peer):
        return pltpu.make_async_remote_copy(
            done.at[1, slot, c],
            back_on.at[i, at, c],
            back_on_send_sem.at[slot, c],
            back_on_recv_sem.at[i, at, c],
            {"exp": base + peer},
            MESH,
        )

    def each_peer(action):
        def one(j, _):
            action(flip(place, half - 1 - j, bits))
            return 0

        lax.fori_loop(0, half - 1, one, 0)

    def each_slot(action, here=None):
        def one(n, _):
            at, i = proxy_place(lax.div(n, 2)), lax.rem(n, 2)

            @pl.when(at != place)
            def _():
                action(n, at, i)

            if here is not None:

                @pl.when(at == place)
                def _():
                    here(n, i)

            return 0

        lax.fori_loop(0, half, one, 0)

    def picked(at, source):
        rows = dot(pick[at].reshape(half * cap, block_len), source[...])
        return rows.astype(BF16).reshape(half, cap, tile)

    def activate(gate_part, up_part):
        return (gate_part / (1.0 + jnp.exp(-gate_part)) * up_part).astype(BF16)

    def each_hidden(action):
        def one(n, _):
            action(pl.ds(pl.multiple_of(n * 256, 256), 256))
            return 0

        lax.fori_loop(0, ff // 256, one, 0)

    def run_up():
        def one(cols):
            gate_part = up_part = 0.0
            for c in range(parts):
                rows = recv[0, :, c].reshape(half * cap, tile)
                gate_part = gate_part + dot(rows, wg[part_cols(c), cols])
                up_part = up_part + dot(rows, wu[part_cols(c), cols])
            act[0, :, cols] = activate(gate_part, up_part)

        each_hidden(one)

    def add_up(c):
        each_slot(lambda n, at, i: go_on_copy(c, i, at, n).wait_recv())

        def one(cols):
            rows = recv[1, :, c].reshape(half * cap, tile)
            gate_part = dot(rows, wg[part_cols(c), cols])
            up_part = dot(rows, wu[part_cols(c), cols])
            if c > 0:
                gate_part = gate_part + gate_sum[:, cols]
                up_part = up_part + up_sum[:, cols]
            if c < parts - 1:
                gate_sum[:, cols] = gate_part
                up_sum[:, cols] = up_part
            else:
                act[1, :, cols] = activate(gate_part, up_part)

        each_hidden(one)

    def run_down(at, c):
        rows = dot(act[at], wd[:, part_cols(c)]).astype(BF16)
        done[at, :, c] = rows.reshape(half, cap, tile)

    for c in range(parts):
        normed[c] = (h_res[:, part_cols(c)] * scale * norm_gain_ref[:, part_cols(c)]).astype(BF16)
        relay_copy(c, line).start()
    slots(0, info)
    for c in range(parts):
        send[:, c] = picked(0, normed.at[c])
        recv[0, place, c] = send[place, c]
    each_peer(lambda peer: go_copy(peer, place).start())
    @pl.when(proxy)
    def _():
        for i in range(2):
            pltpu.make_async_remote_copy(
                info, info_in.at[i], info_send_sem, info_recv_sem.at[i], {"exp": target}, MESH
            ).wait_recv()
            slots(1 + i, info_in.at[i])

    for copy in weight_copies:
        copy.wait()

    for c in range(parts):
        @pl.when(proxy)
        def _(c=c):
            for i in range(2):
                slot_here = low * 2 + i
                relay_copy(c, i).wait_recv()
                send_on[i, :, c] = picked(1 + i, relay.at[i, c])
                recv[1, slot_here, c] = send_on[i, place, c]
                each_peer(lambda peer: go_on_copy(c, i, peer, slot_here).start())

        if c >= LAG:
            add_up(c - LAG)

    for c in range(parts - LAG, parts):
        add_up(c)
    for c in range(parts):
        run_down(1, c)

        def keep(n, i, c=c):
            back_on[i, place, c] = done[1, n, c]

        each_slot(lambda n, at, i, c=c: back_on_copy(c, i, n, place, at).start(), keep)

    def serve_own():
        each_peer(lambda peer: go_copy(peer, peer).wait_recv())
        run_up()
        for c in range(parts):
            run_down(0, c)
            back[place, c] = done[0, place, c]
        each_peer(lambda peer: back_copy(peer, place).start())

    @pl.when(jnp.logical_not(proxy))
    def _():
        serve_own()

    @pl.when(proxy)
    def _():
        for c in range(parts):
            if c == 2:
                serve_own()
            for i in range(2):
                each_peer(lambda peer: back_on_copy(c, i, peer, peer, peer).wait_recv())
                rows = back_on[i, :, c].reshape(half * cap, tile)
                part_out[i, c] = dot(mix[1 + i], rows).astype(BF16)
                part_copy(c, i).start()

    each_peer(lambda peer: back_copy(peer, peer).wait_recv())
    for c in range(parts):
        h_res[:, part_cols(c)] += dot(mix[0], back[:, c].reshape(half * cap, tile))
    for c in range(parts):
        part_copy(c, 0).wait_recv()
        out_ref[:, part_cols(c)] = (h_res[:, part_cols(c)] + part_in[c].astype(F32)).astype(BF16)

    info_copy.wait_send()
    each_peer(lambda peer: go_copy(peer, place).wait_send())
    each_peer(lambda peer: back_copy(peer, place).wait_send())
    for c in range(parts):
        relay_copy(c, line).wait_send()
        each_slot(lambda n, at, i, c=c: back_on_copy(c, i, n, place, at).wait_send())

    @pl.when(proxy)
    def _():
        for c in range(parts):
            for i in range(2):
                part_copy(c, i).wait_send()
                each_peer(lambda peer: go_on_copy(c, i, peer, 0).wait_send())

    @pl.when(core == 0)
    def _():
        log_copy(seq + 1).wait_send()
        for g in range(GROUPS):
            pair_copy(seq + 1, g).wait_send()

    @pl.when((core == 1) & (chip < seqs // 2 - 1))
    def _():
        for g in range(GROUPS):
            state_copy(g).wait_send()

    for g in range(GROUPS):

        @pl.when((chip > 0) & (core == g % 2))
        def _(g=g):
            pass_copy(g).wait_send()


def per_device(
    layer_input,
    queries,
    keys_in,
    values_in,
    decay_rate,
    attn_gain,
    norm_gain,
    expert_ids,
    gate_levels,
    w_gate,
    w_up,
    w_down,
):
    block_len, width = layer_input.shape[1:]
    heads = decay_rate.shape[2]
    dh = width // heads
    top = expert_ids.shape[2]
    ff = w_gate.shape[2]
    owners = lax.axis_size("exp")
    seqs = lax.axis_size("seq")
    half = owners // 2
    cap = -(-(3 * block_len // owners) // 16) * 16
    tile = width // PARTS
    vmem = pl.BlockSpec(memory_space=pltpu.VMEM)
    hbm = pl.BlockSpec(memory_space=pl.ANY)
    state = pltpu.VMEM((heads, dh, dh), BF16)
    rows = pltpu.VMEM((half, PARTS, cap, tile), BF16)
    two_rows = pltpu.VMEM((2, half, PARTS, cap, tile), BF16)
    columns = pltpu.VMEM((PARTS, block_len, tile), BF16)
    two_columns = pltpu.VMEM((2, PARTS, block_len, tile), BF16)
    known = pltpu.VMEM((2, owners, block_len), F32)
    dma = pltpu.SemaphoreType.DMA
    out = pl.pallas_call(
        functools.partial(layer_kernel, (owners, cap, seqs, heads, top)),
        out_shape=jax.ShapeDtypeStruct((block_len, width), BF16),
        in_specs=[vmem] * 9 + [hbm] * 3,
        out_specs=vmem,
        scratch_shapes=[
            pltpu.VMEM((width, ff), BF16),
            pltpu.VMEM((width, ff), BF16),
            pltpu.VMEM((ff, width), BF16),
            pltpu.VMEM((block_len, heads), F32),
            pltpu.VMEM((heads, block_len), F32),
            pltpu.VMEM((heads, dh), F32),
            pltpu.VMEM((heads, dh), F32),
            pltpu.VMEM((heads, dh, dh), F32),
            state,
            state,
            state,
            state,
            pltpu.VMEM((block_len, width), F32),
            columns,
            two_columns,
            known,
            pltpu.VMEM((2, 2, owners, block_len), F32),
            pltpu.VMEM((3, half, cap, block_len), BF16),
            pltpu.VMEM((3, block_len, half * cap), BF16),
            rows,
            two_rows,
            two_rows,
            pltpu.VMEM((2, half * cap, ff), BF16),
            pltpu.VMEM((half * cap, ff), F32),
            pltpu.VMEM((half * cap, ff), F32),
            two_rows,
            rows,
            two_rows,
            two_columns,
            columns,
            dma((3,)),
            dma((2, GROUPS)),
            dma((2,)),
            dma((GROUPS,)),
            dma((GROUPS,)),
            dma((GROUPS,)),
            dma,
            dma((2,)),
            dma((PARTS,)),
            dma((2, PARTS)),
            dma((half,)),
            dma((half,)),
            dma((2, half, PARTS)),
            dma((half, PARTS)),
            dma((half,)),
            dma((half,)),
            dma((half, PARTS)),
            dma((2, half, PARTS)),
            dma((2, PARTS)),
            dma((PARTS,)),
        ],
        compiler_params=pltpu.CompilerParams(
            collective_id=0, has_side_effects=True, vmem_limit_bytes=56 * 1024 * 1024
        ),
    )(
        layer_input[0],
        queries[0],
        keys_in[0],
        values_in[0],
        decay_rate[0].T,
        attn_gain[None],
        norm_gain[None],
        expert_ids[0].T,
        gate_levels[0].T,
        w_gate[0],
        w_up[0],
        w_down[0],
    )
    return out[None]


def solution(mesh):
    tokens = P("exp", "seq", None)
    experts = P("exp", None, None)
    return jax.shard_map(
        per_device,
        mesh=mesh,
        in_specs=(tokens,) * 5 + (P(), P()) + (tokens,) * 2 + (experts,) * 3,
        out_specs=tokens,
        check_vma=False,
    )
```
